32 devices in a mesh: ctx: 4 (over x, core), vocab: 8 (over z, y).
Axes of the slice: x: 2, y: 2, z: 4, core: 2. Of those that a mesh axis runs over, the one named last changes fastest.
Arguments:
- hidden_state: bfloat16 [512, 7168], P('ctx'), may hold values from -50 to 50
- embedded_next: bfloat16 [512, 7168], P('ctx'), may hold values from -50 to 50
- gain_hidden: float32 [7168], replicated, may hold values from 0.1 to 1.9
- gain_embed: float32 [7168], replicated, may hold values from 0.1 to 1.9
- proj_hidden: bfloat16 [7168, 7168], P('ctx', 'vocab'), may hold values from -0.0625 to 0.0625
- proj_embed: bfloat16 [7168, 7168], P('ctx', 'vocab'), may hold values from -0.0625 to 0.0625
- final_gain: float32 [7168], P('vocab'), may hold values from 0.1 to 1.9
- head: bfloat16 [65536, 7168], P(('ctx', 'vocab')), may hold values from -0.4375 to 0.4375
- targets: int32 [512], replicated, may hold values from 0 to 65535
- loss_mask: int32 [512], replicated, may hold values 0 or 1
Outputs:
- mean_loss: float32 [], replicated
- grad_hidden: bfloat16 [512, 7168], P('ctx', 'vocab')
- grad_embed: bfloat16 [512, 7168], P('ctx', 'vocab')
- grad_gain_hidden: float32 [7168], P('vocab')
- grad_gain_embed: float32 [7168], P('vocab')
- grad_proj_hidden: bfloat16 [7168, 7168], P('ctx', 'vocab')
- grad_proj_embed: bfloat16 [7168, 7168], P('ctx', 'vocab')
- grad_final_gain: float32 [7168], P('vocab')
- grad_head: bfloat16 [65536, 7168], P(('ctx', 'vocab'))
The draws below stay inside these ranges and needn't reach their ends.
All inputs are finite; a program needn't handle non-finite values.
Results may differ from the reference program's by a relative error of at most 0.023.
Values may be sent and summed in bfloat16 or wider, within the bound.
No kernel may reach another device: no remote copies, remote signals or barrier semaphores. Data moves between devices by JAX's collectives and lax.ppermute only.
A program may use at most 256 MiB of HBM per device.

```python
import math
import jax
import jax.numpy as jnp
from jax import lax

D = 7168
VOCAB = 65536
TOKENS = 512


def spread_factors(key, row_total, col_total):
    row_key, col_key = jax.random.split(key)
    row_factor = jnp.exp(jax.random.uniform(row_key, (row_total, 1), jnp.float32) * math.log(10.0))
    col_factor = jnp.exp(jax.random.uniform(col_key, (1, col_total), jnp.float32) * math.log(10.0))
    return row_factor * col_factor


def draw_hidden_state(key, part):
    key = jax.random.fold_in(key, 11)
    base_key, scale_key = jax.random.split(key)
    base = jnp.clip(jax.random.normal(base_key, (TOKENS, D), jnp.float32), -5.0, 5.0)
    return (base * spread_factors(scale_key, TOKENS, D) * 0.1).astype(jnp.bfloat16)


def draw_embedded_next(key, part):
    key = jax.random.fold_in(key, 23)
    base_key, scale_key = jax.random.split(key)
    base = jnp.clip(jax.random.normal(base_key, (TOKENS, D), jnp.float32), -5.0, 5.0)
    return (base * spread_factors(scale_key, TOKENS, D) * 0.1).astype(jnp.bfloat16)


def set_ends(drawn, stream_key, least, largest):
    extent = drawn.shape
    place = [jax.random.randint(jax.random.fold_in(stream_key, axis), (), 0, extent[axis]) for axis in range(len(extent))]
    drawn = drawn.at[tuple(place)].set(least)
    longest = extent.index(max(extent))
    place[longest] = (place[longest] + 1) % extent[longest]
    return drawn.at[tuple(place)].set(largest)


def strengthened(array, own_key, source, target, parts, factor):
    owner, partner = [(jnp.arange(array.shape[position]) // (array.shape[position] // parts)).reshape([-1 if axis == position else 1 for axis in range(array.ndim)]) for position in (source, target)]
    chosen = jax.random.permutation(own_key, parts)[partner]
    strong = (owner == chosen) | (owner == (partner + parts // 2) % parts)
    return jnp.where(strong, factor * array, array)


def block_scale(key, shape, cuts, low, top_value):
    loudness = 1.0
    for axis_at, parts in cuts:
        steps = jax.random.uniform(jax.random.fold_in(jax.random.fold_in(key, 6), axis_at), (parts,), jnp.float32, low / len(cuts), top_value / len(cuts))
        loudness = loudness * jnp.repeat(jnp.exp(steps), shape[axis_at] // parts).reshape((-1,) + (1,) * (len(shape) - 1 - axis_at))
    return loudness


def bell_draw(stream_key, shape, spread, limit, cuts=(), held_as=jnp.bfloat16):
    entries = spread * jax.random.normal(stream_key, shape, jnp.float32)
    if cuts:
        entries = entries * block_scale(stream_key, shape, cuts, -0.22, 0.18)
    return jnp.clip(entries, -limit, limit).astype(held_as)


def noise_with(key, shape, deviation, limit, cuts, heavy, kind=jnp.bfloat16):
    array = deviation * jax.random.normal(key, shape, jnp.float32)
    if cuts:
        array = array * block_scale(key, shape, cuts, -0.22, 0.18)
    return jnp.clip(strengthened(array, jax.random.fold_in(key, 3), *heavy), -limit, limit).astype(kind)


def setup_inputs(seed: int = 0) -> dict:
    splits = jax.random.split(jax.random.key(seed), 11)
    return {
        "hidden_state": draw_hidden_state(jax.random.fold_in(splits[10], 71), 0),
        "embedded_next": draw_embedded_next(jax.random.fold_in(splits[10], 71), 0),
        "gain_hidden": jnp.clip(1.0 + 0.18 * jax.random.normal(splits[2], (D,), jnp.float32), 0.1, 1.9),
        "gain_embed": jnp.clip(1.0 + 0.18 * jax.random.normal(splits[3], (D,), jnp.float32), 0.1, 1.9),
        "proj_hidden": bell_draw(splits[4], (D, D), D ** -0.5, 0.0625, ((0, 4), (1, 8))),
        "proj_embed": bell_draw(splits[5], (D, D), D ** -0.5, 0.0625, ((0, 4), (1, 8))),
        "final_gain": jnp.clip(1.0 + 0.18 * jax.random.normal(splits[6], (D,), jnp.float32), 0.1, 1.9),
        "head": noise_with(splits[7], (VOCAB, D), (D // 9) ** -0.5, 0.4375, ((0, 32),), (0, 1, 32, 2.75)),
        "targets": set_ends(jax.random.randint(splits[8], (TOKENS,), 0, VOCAB), jax.random.fold_in(splits[8], 1), 0, VOCAB - 1).astype(jnp.int32),
        "loss_mask": set_ends((jax.random.randint(splits[9], (TOKENS,), 0, 4) < 3).astype(jnp.int32), jax.random.fold_in(splits[9], 1), 0, 1),
    }


EPSILON = 1e-06

def scale_of(values):
    return lax.rsqrt(lax.optimization_barrier(jnp.mean(values * values, axis=-1, keepdims=True)) + EPSILON)

def reference(hidden_state, embedded_next, gain_hidden, gain_embed, proj_hidden, proj_embed, final_gain, head, targets, loss_mask):
    hidden_wide = hidden_state.astype(jnp.float32)
    embed_wide = embedded_next.astype(jnp.float32)
    hidden_scale = scale_of(hidden_wide)
    embed_scale = scale_of(embed_wide)
    normed_hidden = (hidden_wide * hidden_scale * gain_hidden).astype(jnp.bfloat16)
    normed_embed = (embed_wide * embed_scale * gain_embed).astype(jnp.bfloat16)
    projected = jnp.dot(normed_hidden, proj_hidden, preferred_element_type=jnp.float32) + jnp.dot(normed_embed, proj_embed, preferred_element_type=jnp.float32)
    row_scale = scale_of(projected)
    normed_rows = (projected * row_scale * final_gain).astype(jnp.bfloat16)
    logits = jnp.dot(normed_rows, head.T, preferred_element_type=jnp.float32)
    log_total = jnp.log(lax.optimization_barrier(jnp.sum(jnp.exp(logits), axis=-1)))
    is_target = targets[:, None] == jnp.arange(VOCAB, dtype=jnp.int32)[None, :]
    target_logit = lax.optimization_barrier(jnp.sum(jnp.where(is_target, logits, jnp.float32(0.0)), axis=-1))
    mask_weight = loss_mask.astype(jnp.float32)
    mean_loss = jnp.sum(mask_weight * (log_total - target_logit)) / TOKENS
    probs = jnp.exp(logits - log_total[:, None])
    logit_grad = (mask_weight[:, None] * (probs - is_target.astype(jnp.float32))).astype(jnp.bfloat16)
    block_size = math.gcd(VOCAB, 4096)
    block_count = VOCAB // block_size
    grad_blocks = logit_grad.reshape(TOKENS, block_count, block_size).transpose(1, 0, 2)
    head_blocks = head.reshape(block_count, block_size, D)

    def head_block(carry, pieces):
        grad_piece, weight_piece = pieces
        carry = carry + jnp.dot(grad_piece, weight_piece, preferred_element_type=jnp.float32)
        return (carry, jnp.dot(grad_piece.T, normed_rows, preferred_element_type=jnp.float32).astype(jnp.bfloat16))
    normed_grad, head_parts = lax.scan(head_block, jnp.zeros((TOKENS, D), jnp.float32), (grad_blocks, head_blocks))
    grad_head = head_parts.reshape(VOCAB, D)
    grad_final_gain = lax.optimization_barrier(jnp.sum(normed_grad * projected * row_scale, axis=0))
    scaled_grad = normed_grad * final_gain
    row_dot = lax.optimization_barrier(jnp.sum(scaled_grad * projected, axis=-1, keepdims=True))
    proj_grad = (row_scale * scaled_grad - projected * (row_scale * row_scale * row_scale) * (row_dot / D)).astype(jnp.bfloat16)
    grad_proj_hidden = jnp.dot(normed_hidden.T, proj_grad, preferred_element_type=jnp.float32).astype(jnp.bfloat16)
    grad_proj_embed = jnp.dot(normed_embed.T, proj_grad, preferred_element_type=jnp.float32).astype(jnp.bfloat16)
    hidden_back = jnp.dot(proj_grad, proj_hidden.T, preferred_element_type=jnp.float32)
    embed_back = jnp.dot(proj_grad, proj_embed.T, preferred_element_type=jnp.float32)
    grad_gain_hidden = lax.optimization_barrier(jnp.sum(hidden_back * hidden_wide * hidden_scale, axis=0))
    grad_gain_embed = lax.optimization_barrier(jnp.sum(embed_back * embed_wide * embed_scale, axis=0))
    hidden_dot = lax.optimization_barrier(jnp.sum(hidden_back * gain_hidden * hidden_wide, axis=-1, keepdims=True))
    embed_dot = lax.optimization_barrier(jnp.sum(embed_back * gain_embed * embed_wide, axis=-1, keepdims=True))
    grad_hidden = (hidden_scale * (hidden_back * gain_hidden) - hidden_wide * (hidden_scale * hidden_scale * hidden_scale) * (hidden_dot / D)).astype(jnp.bfloat16)
    grad_embed = (embed_scale * (embed_back * gain_embed) - embed_wide * (embed_scale * embed_scale * embed_scale) * (embed_dot / D)).astype(jnp.bfloat16)
    return (mean_loss, grad_hidden, grad_embed, grad_gain_hidden, grad_gain_embed, grad_proj_hidden, grad_proj_embed, grad_final_gain, grad_head)
```

```python
import jax
import jax.numpy as jnp
from jax import lax
from jax.sharding import PartitionSpec as P

EPSILON = 1e-06
PARTS = 2
F32 = jnp.float32
BF16 = jnp.bfloat16


class Dim:
    def __init__(self, axis, size, n, stride):
        self.axis, self.size, self.n, self.stride = axis, size, n, stride

    def place(self):
        return (lax.axis_index(self.axis) // self.stride) % self.n

    def move(self, value, target):
        pairs = []
        for index in range(self.size):
            here = (index // self.stride) % self.n
            there = target(here)
            if there is not None and 0 <= there < self.n:
                pairs.append((index, index + (there - here) * self.stride))
        return lax.ppermute(value, self.axis, pairs)

    def swap(self, value, bit):
        return self.move(value, lambda here: here ^ bit)

    def turn(self, value, by):
        return self.move(value, lambda here: (here + by) % self.n)


def butterfly(value, dims):
    for dim in dims:
        bit = 1
        while bit < dim.n:
            value = value + dim.swap(value, bit)
            bit *= 2
    return value


def line_gather(value, dim):
    n, here = dim.n, dim.place()
    if n == 2:
        other = dim.swap(value, 1)
        return [jnp.where(here == 0, value, other), jnp.where(here == 0, other, value)]
    up, down = [value], [value]
    for step in range(1, n):
        up.append(dim.move(up[-1], lambda k: k + 1 if k >= step - 1 else None))
        down.append(dim.move(down[-1], lambda k: k - 1 if k <= n - step else None))
    out = []
    for spot in range(n):
        piece = value
        for step in range(1, n):
            if spot + step < n:
                piece = jnp.where(here == spot + step, up[step], piece)
            if spot - step >= 0:
                piece = jnp.where(here == spot - step, down[step], piece)
        out.append(piece)
    return out


def line_scatter(chunks, dim):
    n, here = dim.n, dim.place()

    def pick(at):
        return lax.dynamic_index_in_dim(chunks, jnp.clip(at, 0, n - 1), 0, keepdims=False)

    if n == 2:
        return pick(here).astype(F32) + dim.swap(pick(1 - here), 1).astype(F32)
    up = down = None
    for step in range(1, n):
        up_send, down_send = pick(here + n - step), pick(here - n + step)
        if up is not None:
            up_send = (up_send.astype(F32) + up.astype(F32)).astype(BF16)
            down_send = (down_send.astype(F32) + down.astype(F32)).astype(BF16)
        up = dim.move(up_send, lambda k: k + 1 if k <= step - 1 else None)
        down = dim.move(down_send, lambda k: k - 1 if k >= n - step else None)
    return pick(here).astype(F32) + up.astype(F32) + down.astype(F32)


def contract_first(left, right):
    return lax.dot_general(left, right, (((0,), (0,)), ((), ())), preferred_element_type=F32)


def contract_last(left, right):
    return lax.dot_general(left, right, (((1,), (1,)), ((), ())), preferred_element_type=F32)


def dot(left, right):
    return jnp.dot(left, right, preferred_element_type=F32)


def cut(array, start, width, axis):
    return lax.dynamic_slice_in_dim(array, start, width, axis)


def local(
    hidden_state,
    embedded_next,
    gain_hidden,
    gain_embed,
    proj_hidden,
    proj_embed,
    final_gain,
    head,
    targets,
    loss_mask,
):
    nc, nv = lax.axis_size("ctx"), lax.axis_size("vocab")
    nx, va = nc // 2, 4
    vb = nv // va
    core = Dim("ctx", nc, 2, 1)
    dim_x = Dim("ctx", nc, nx, 2)
    dim_b = Dim("vocab", nv, vb, 1)
    dim_a = Dim("vocab", nv, va, vb)
    every = (core, dim_x, dim_b, dim_a)
    own, slot = lax.axis_index("ctx"), lax.axis_index("vocab")
    x, c, a, b = own // 2, own % 2, slot // vb, slot % vb
    even = b % 2 == 0

    width = hidden_state.shape[1]
    block = hidden_state.shape[0]
    token_total = targets.shape[0]
    feat, cols = proj_hidden.shape
    rows = block // PARTS
    half = rows // 2
    vocab_local = head.shape[0]

    def relative_place(block_index):
        return (c ^ (block_index % 2)) * nx + (x - block_index // 2) % nx

    order = jnp.stack([relative_place(jnp.int32(i)) for i in range(nc)])
    to_absolute = order[:, None] == jnp.arange(nc, dtype=jnp.int32)[None, :]

    def absolute(value):
        value = value.reshape(value.shape[:-1] + (nc, rows))
        return jnp.sum(jnp.where(to_absolute[:, :, None], value[..., None, :, :], 0), axis=-2)

    def relative(value):
        value = jnp.sum(jnp.where(to_absolute[:, :, None], value[..., :, None, :], 0), axis=-3)
        return value.reshape(value.shape[:-2] + (nc * rows,))

    def gather_x(value):
        return jnp.stack([value] + [dim_x.turn(value, r) for r in range(1, nx)])

    hidden_wide, embed_wide = hidden_state.astype(F32), embedded_next.astype(F32)
    scales = lax.rsqrt(
        jnp.stack(
            [jnp.mean(hidden_wide * hidden_wide, axis=-1), jnp.mean(embed_wide * embed_wide, axis=-1)]
        )
        + EPSILON
    )
    scales_x = gather_x(scales)
    scales_all = jnp.concatenate([scales_x, core.swap(scales_x, 1)])
    gain_h_own = cut(gain_hidden, own * feat, feat, 0)
    gain_e_own = cut(gain_embed, own * feat, feat, 0)

    def inputs(part):
        hid = hidden_state[part * rows : (part + 1) * rows]
        emb = embedded_next[part * rows : (part + 1) * rows]
        hid_list = [cut(hid, x * 2 * feat, 2 * feat, 1)]
        emb_list = [cut(emb, x * 2 * feat, 2 * feat, 1)]
        for r in range(1, nx):
            start = ((x + r) % nx) * 2 * feat
            send = jnp.where(even, cut(hid, start, 2 * feat, 1), cut(emb, start, 2 * feat, 1))
            got = dim_x.turn(send, r)
            twin = dim_b.swap(got, 1)
            hid_list.append(jnp.where(even, got, twin))
            emb_list.append(jnp.where(even, twin, got))
        out = []
        for kind, (pieces, gain) in enumerate(((hid_list, gain_h_own), (emb_list, gain_e_own))):
            mine = [cut(piece, c * feat, feat, 1) for piece in pieces]
            theirs = [core.swap(cut(piece, (1 - c) * feat, feat, 1), 1) for piece in pieces]
            raw = jnp.concatenate(mine + theirs).astype(F32)
            scale = scales_all[:, kind, part * rows : (part + 1) * rows].reshape(nc * rows, 1)
            out.append((raw * scale * gain).astype(BF16))
        return out

    def project(normed_h, normed_e):
        part_h, part_e = dot(normed_h, proj_hidden), dot(normed_e, proj_embed)
        total = part_h + part_e
        mine, theirs = total[: nx * rows], total[nx * rows :].astype(BF16)
        mine = mine + core.swap(theirs, 1).astype(F32)
        projected = mine[:rows]
        for r in range(1, nx):
            piece = mine[r * rows : (r + 1) * rows].astype(BF16)
            projected = projected + dim_x.turn(piece, -r).astype(F32)
        return projected, part_h, part_e

    def spread(projected):
        squares = jnp.sum(projected * projected, axis=-1)
        mine = jnp.arange(nc, dtype=jnp.int32)[:, None] == own
        squares = butterfly(jnp.where(mine, squares[None, :], 0.0), every)
        row_scale = relative(lax.rsqrt(squares / width + EPSILON))
        piece = (projected * final_gain).astype(BF16)
        along = jnp.stack(line_gather(piece, dim_a))
        first = jnp.stack(line_gather(along[:, :half], dim_b))
        first = gather_x(first)
        second = gather_x(along[:, half:])
        second = jnp.stack(line_gather(second, dim_b), axis=1)
        lines = []
        for r in range(nx):
            for source in (first, second):
                lines.append(
                    jnp.concatenate(
                        [source[r, q, p] for p in range(va) for q in range(vb)], axis=1
                    )
                )
        mine = jnp.concatenate(lines)
        return jnp.concatenate([mine, core.swap(mine, 1)]), row_scale

    vocab_ids = (own * nv + slot) * vocab_local + lax.iota(jnp.int32, vocab_local)
    mask_weight = loss_mask.astype(F32).reshape(nc, block)
    target_blocks = targets.reshape(nc, block)

    def cross_entropy(part, gathered, row_scale):
        logits = contract_last(gathered, head) * row_scale[:, None]
        target = relative(target_blocks[:, part * rows : (part + 1) * rows])
        mask = relative(mask_weight[:, part * rows : (part + 1) * rows])
        is_target = target[:, None] == vocab_ids[None, :]
        power = jnp.exp(logits)
        sums = jnp.stack(
            [
                jnp.sum(power, axis=-1),
                jnp.sum(power * (logits * F32(1.0 / 256.0)), axis=-1),
                jnp.sum(jnp.where(is_target, logits, F32(0.0)), axis=-1),
            ]
        )
        sums = butterfly(absolute(sums), every)
        total, weighted, target_logit = sums[0], sums[1], sums[2]
        log_total = jnp.log(total)
        loss = jnp.sum(
            mask_weight[:, part * rows : (part + 1) * rows] * (log_total - target_logit)
        )
        scaled_dot = mask * relative(weighted / total * F32(256.0) - target_logit)
        probs = jnp.exp(logits - relative(log_total)[:, None])
        scaled_grad = ((mask * row_scale)[:, None] * (probs - is_target.astype(F32))).astype(BF16)
        return scaled_grad, scaled_dot, loss

    def column_chunk(value, place):
        return jnp.stack([cut(value, (p * vb + place) * cols, cols, value.ndim - 1) for p in range(va)])

    def collect(scaled_grad):
        partial = dot(scaled_grad, head)
        mine, theirs = partial[: nx * rows], partial[nx * rows :].astype(BF16)
        mine = (mine + core.swap(theirs, 1).astype(F32)).astype(BF16)
        mine = mine.reshape(nx, rows, width)
        first = mine[0, :half].astype(F32)
        for r in range(1, nx):
            first = first + dim_x.turn(mine[r, :half], -r).astype(F32)
        first = first.astype(BF16)
        kept = column_chunk(first, b).astype(F32)
        for r in range(1, vb):
            kept = kept + dim_b.turn(column_chunk(first, (b + r) % vb), r).astype(F32)
        first = kept.astype(BF16)
        second = mine[:, half:]
        kept = column_chunk(second, b).astype(F32)
        for r in range(1, vb):
            kept = kept + dim_b.turn(column_chunk(second, (b + r) % vb), r).astype(F32)
        second = kept.astype(BF16)
        kept = second[:, 0].astype(F32)
        for r in range(1, nx):
            kept = kept + dim_x.turn(second[:, r], -r).astype(F32)
        second = kept.astype(BF16)
        summed = line_scatter(jnp.concatenate([first, second], axis=1), dim_a).astype(BF16)
        along = gather_x(summed)
        along = jnp.concatenate([along, core.swap(along, 1)])
        return along.reshape(nc * rows, cols)

    def final_move(value):
        pairs = []
        ratio = nv // nc
        for i in range(nc):
            for j in range(nv):
                pairs.append((i * nv + j, (j // ratio) * nv + i * ratio + j % ratio))
        return lax.ppermute(value, ("ctx", "vocab"), pairs)

    def back(proj_grad, weight):
        def product(place):
            picked = [
                cut(proj_grad, relative_place((p * vb + place) // 2) * rows, rows, 0)
                for p in range(va)
            ]
            weight_half = cut(weight, (place % 2) * cols, cols, 0)
            return contract_last(jnp.concatenate(picked), weight_half)

        sends = [dim_b.swap(product(b ^ r).astype(BF16), r) for r in range(1, vb)]
        kept = product(b)
        for got in sends:
            kept = kept + got.astype(F32)
        kept = kept.astype(BF16).reshape(va, rows, cols)
        return final_move(line_scatter(kept, dim_a).astype(BF16)).astype(F32)

    normed_h, normed_e, halves, gathered, row_scales = [], [], [], [], []
    for part in range(PARTS):
        nh, ne = inputs(part)
        projected, part_h, part_e = project(nh, ne)
        rows_all, row_scale = spread(projected)
        normed_h.append(nh)
        normed_e.append(ne)
        halves.append((part_h, part_e))
        gathered.append(rows_all)
        row_scales.append(row_scale)

    logit_grads, scaled_dots = [], []
    mean_loss = F32(0.0)
    for part in range(PARTS):
        scaled_grad, scaled_dot, loss = cross_entropy(part, gathered[part], row_scales[part])
        logit_grads.append(scaled_grad)
        scaled_dots.append(scaled_dot)
        mean_loss = mean_loss + loss
    mean_loss = mean_loss / token_total

    proj_grads, hidden_backs, embed_backs, dots = [], [], [], []
    grad_final_gain = jnp.zeros((cols,), F32)
    for part in range(PARTS):
        scaled = collect(logit_grads[part]).astype(F32)
        projected = cut(gathered[part], slot * cols, cols, 1).astype(F32) / final_gain
        grad_final_gain = grad_final_gain + jnp.sum(scaled * projected, axis=0)
        coefficient = row_scales[part] * row_scales[part] * scaled_dots[part] / width
        proj_grad = (scaled * final_gain - projected * coefficient[:, None]).astype(BF16)
        proj_grads.append(proj_grad)
        wide = proj_grad.astype(F32)
        part_h, part_e = halves[part]
        sums = jnp.stack([jnp.sum(wide * part_h, axis=-1), jnp.sum(wide * part_e, axis=-1)])
        sums = butterfly(absolute(sums), every)
        dots.append(lax.dynamic_index_in_dim(sums, own, 1, keepdims=False))
        hidden_backs.append(back(proj_grad, proj_hidden))
        embed_backs.append(back(proj_grad, proj_embed))

    rows_all = jnp.concatenate(gathered)
    grad_head = contract_first(jnp.concatenate(logit_grads), rows_all).astype(BF16)
    proj_grad = jnp.concatenate(proj_grads)
    wide_h = contract_first(jnp.concatenate(normed_h), proj_grad)
    wide_e = contract_first(jnp.concatenate(normed_e), proj_grad)
    grad_proj_hidden, grad_proj_embed = wide_h.astype(BF16), wide_e.astype(BF16)
    gains = jnp.stack(
        [
            jnp.sum(wide_h * proj_hidden.astype(F32), axis=1) / gain_h_own,
            jnp.sum(wide_e * proj_embed.astype(F32), axis=1) / gain_e_own,
        ]
    )
    gains = butterfly(gains, (dim_b, dim_a))
    gains = final_move(cut(gains, (b % 2) * cols, cols, 1))

    def finish(backs, wide, gain, kind):
        back_all = jnp.concatenate(backs)
        scale = scales[kind][:, None]
        dot_all = jnp.concatenate([pair[kind] for pair in dots])[:, None]
        source = cut(wide, slot * cols, cols, 1).astype(F32)
        gain_piece = cut(gain, slot * cols, cols, 0)
        return (
            scale * (back_all * gain_piece) - source * (scale * scale) * (dot_all / width)
        ).astype(BF16)

    return (
        mean_loss,
        finish(hidden_backs, hidden_state, gain_hidden, 0),
        finish(embed_backs, embedded_next, gain_embed, 1),
        gains[0],
        gains[1],
        grad_proj_hidden,
        grad_proj_embed,
        grad_final_gain,
        grad_head,
    )


def solution(mesh):
    in_specs = (
        P("ctx", None),
        P("ctx", None),
        P(),
        P(),
        P("ctx", "vocab"),
        P("ctx", "vocab"),
        P("vocab"),
        P(("ctx", "vocab"), None),
        P(),
        P(),
    )
    out_specs = (
        P(),
        P("ctx", "vocab"),
        P("ctx", "vocab"),
        P("vocab"),
        P("vocab"),
        P("ctx", "vocab"),
        P("ctx", "vocab"),
        P("vocab"),
        P(("ctx", "vocab"), None),
    )
    return jax.shard_map(local, mesh=mesh, in_specs=in_specs, out_specs=out_specs, check_vma=False)
```

```python
import jax
import jax.numpy as jnp
from jax import lax
from jax.sharding import PartitionSpec as P

EPSILON = 1e-06
PARTS = 1
F32 = jnp.float32
BF16 = jnp.bfloat16


class Dim:
    def __init__(self, axis, size, n, stride):
        self.axis, self.size, self.n, self.stride = axis, size, n, stride

    def place(self):
        return (lax.axis_index(self.axis) // self.stride) % self.n

    def move(self, value, target):
        pairs = []
        for index in range(self.size):
            here = (index // self.stride) % self.n
            there = target(here)
            if there is not None and 0 <= there < self.n:
                pairs.append((index, index + (there - here) * self.stride))
        return lax.ppermute(value, self.axis, pairs)

    def swap(self, value, bit):
        return self.move(value, lambda here: here ^ bit)

    def turn(self, value, by):
        return self.move(value, lambda here: (here + by) % self.n)


def halving_scatter(chunks, dim):
    here = dim.place()
    held = {
        offset: lax.dynamic_index_in_dim(chunks, here ^ offset, 0, keepdims=False)
        for offset in range(dim.n)
    }
    bit = 1
    while bit < dim.n:
        send = jnp.stack([held[offset] for offset in range(dim.n) if offset in held and offset & bit])
        got = dim.swap(send, bit)
        keep = [offset for offset in sorted(held) if not offset & bit]
        held = {
            offset: (held[offset].astype(F32) + got[index].astype(F32))
            for index, offset in enumerate(keep)
        }
        bit *= 2
        if bit < dim.n:
            held = {offset: piece.astype(BF16) for offset, piece in held.items()}
    return held[0]


def sum_everywhere(value):
    axes = ("ctx", "vocab")
    count = lax.axis_size("ctx") * lax.axis_size("vocab")
    copies = jnp.broadcast_to(value[None], (count,) + value.shape)
    return jnp.sum(lax.all_to_all(copies, axes, 0, 0, tiled=True), axis=0)


def contract_first(left, right):
    return lax.dot_general(left, right, (((0,), (0,)), ((), ())), preferred_element_type=F32)


def contract_last(left, right):
    return lax.dot_general(left, right, (((1,), (1,)), ((), ())), preferred_element_type=F32)


def dot(left, right):
    return jnp.dot(left, right, preferred_element_type=F32)


def cut(array, start, width, axis):
    return lax.dynamic_slice_in_dim(array, start, width, axis)


def local(
    hidden_state,
    embedded_next,
    gain_hidden,
    gain_embed,
    proj_hidden,
    proj_embed,
    final_gain,
    head,
    targets,
    loss_mask,
):
    nc, nv = lax.axis_size("ctx"), lax.axis_size("vocab")
    nx, va = nc // 2, 4
    vb = nv // va
    core = Dim("ctx", nc, 2, 1)
    dim_x = Dim("ctx", nc, nx, 2)
    dim_b = Dim("vocab", nv, vb, 1)
    dim_a = Dim("vocab", nv, va, vb)
    own, slot = lax.axis_index("ctx"), lax.axis_index("vocab")
    x, c, a, b = own // 2, own % 2, slot // vb, slot % vb

    width = hidden_state.shape[1]
    block = hidden_state.shape[0]
    token_total = targets.shape[0]
    feat, cols = proj_hidden.shape
    rows = block // PARTS
    vocab_local = head.shape[0]

    def relative_place(block_index):
        return (c ^ (block_index % 2)) * nx + (x - block_index // 2) % nx

    order = jnp.stack([relative_place(jnp.int32(i)) for i in range(nc)])
    to_absolute = order[:, None] == jnp.arange(nc, dtype=jnp.int32)[None, :]

    def absolute(value):
        value = value.reshape(value.shape[:-1] + (nc, rows))
        return jnp.sum(jnp.where(to_absolute[:, :, None], value[..., None, :, :], 0), axis=-2)

    def relative(value):
        value = jnp.sum(jnp.where(to_absolute[:, :, None], value[..., :, None, :], 0), axis=-3)
        return value.reshape(value.shape[:-2] + (nc * rows,))

    def gather_x(value):
        return jnp.stack([value] + [dim_x.turn(value, r) for r in range(1, nx)])

    hidden_wide, embed_wide = hidden_state.astype(F32), embedded_next.astype(F32)
    scales = lax.rsqrt(
        jnp.stack(
            [jnp.mean(hidden_wide * hidden_wide, axis=-1), jnp.mean(embed_wide * embed_wide, axis=-1)]
        )
        + EPSILON
    )
    scales_x = gather_x(scales)
    scales_all = jnp.concatenate([scales_x, core.swap(scales_x, 1)])
    gain_all = lax.all_gather(final_gain, "vocab", tiled=True)
    gain_h_own = cut(gain_hidden, own * feat, feat, 0)
    gain_e_own = cut(gain_embed, own * feat, feat, 0)

    def inputs(part):
        hid = hidden_state[part * rows : (part + 1) * rows]
        emb = embedded_next[part * rows : (part + 1) * rows]
        hid_list = [cut(hid, x * 2 * feat, 2 * feat, 1)]
        emb_list = [cut(emb, x * 2 * feat, 2 * feat, 1)]
        for r in range(1, nx):
            start = ((x + r) % nx) * 2 * feat
            hid_list.append(dim_x.turn(cut(hid, start, 2 * feat, 1), r))
            emb_list.append(dim_x.turn(cut(emb, start, 2 * feat, 1), r))
        out = []
        for kind, (pieces, gain) in enumerate(((hid_list, gain_h_own), (emb_list, gain_e_own))):
            mine = [cut(piece, c * feat, feat, 1) for piece in pieces]
            theirs = [core.swap(cut(piece, (1 - c) * feat, feat, 1), 1) for piece in pieces]
            raw = jnp.concatenate(mine + theirs).astype(F32)
            scale = scales_all[:, kind, part * rows : (part + 1) * rows].reshape(nc * rows, 1)
            out.append((raw * scale * gain).astype(BF16))
        return out

    def project(normed_h, normed_e):
        part_h, part_e = dot(normed_h, proj_hidden), dot(normed_e, proj_embed)
        total = part_h + part_e
        mine, theirs = total[: nx * rows], total[nx * rows :].astype(BF16)
        mine = mine + core.swap(theirs, 1).astype(F32)
        projected = mine[:rows]
        for r in range(1, nx):
            piece = mine[r * rows : (r + 1) * rows].astype(BF16)
            projected = projected + dim_x.turn(piece, -r).astype(F32)
        return projected, part_h, part_e

    def spread(projected):
        piece = (projected * final_gain).astype(BF16)
        pieces = lax.all_gather(piece, ("ctx", "vocab"))
        pieces = pieces.reshape(nc, nv, rows, cols)
        lines = []
        for rc in range(2):
            for rx in range(nx):
                at = ((x - rx) % nx) * 2 + (c ^ rc)
                line = lax.dynamic_index_in_dim(pieces, at, 0, keepdims=False)
                lines.append(line.transpose(1, 0, 2).reshape(rows, width))
        gathered = jnp.concatenate(lines)
        plain = gathered.astype(F32) / gain_all
        squares = jnp.sum(plain * plain, axis=-1)
        return gathered, lax.rsqrt(squares / width + EPSILON)

    vocab_ids = (own * nv + slot) * vocab_local + lax.iota(jnp.int32, vocab_local)
    mask_weight = loss_mask.astype(F32).reshape(nc, block)
    target_blocks = targets.reshape(nc, block)

    def cross_entropy(part, gathered, row_scale):
        logits = contract_last(gathered, head) * row_scale[:, None]
        target = relative(target_blocks[:, part * rows : (part + 1) * rows])
        mask = relative(mask_weight[:, part * rows : (part + 1) * rows])
        is_target = target[:, None] == vocab_ids[None, :]
        power = jnp.exp(logits)
        sums = jnp.stack(
            [
                jnp.sum(power, axis=-1),
                jnp.sum(power * (logits * F32(1.0 / 256.0)), axis=-1),
                jnp.sum(jnp.where(is_target, logits, F32(0.0)), axis=-1),
            ]
        )
        sums = sum_everywhere(absolute(sums))
        total, weighted, target_logit = sums[0], sums[1], sums[2]
        log_total = jnp.log(total)
        loss = jnp.sum(
            mask_weight[:, part * rows : (part + 1) * rows] * (log_total - target_logit)
        )
        scaled_dot = mask * relative(weighted / total * F32(256.0) - target_logit)
        probs = jnp.exp(logits - relative(log_total)[:, None])
        scaled_grad = ((mask * row_scale)[:, None] * (probs - is_target.astype(F32))).astype(BF16)
        return scaled_grad, scaled_dot, loss

    def collect(scaled_grad):
        partial = dot(scaled_grad, head).astype(BF16).reshape(nc, rows, width)
        lines = []
        for index in range(nc):
            line = lax.dynamic_index_in_dim(partial, relative_place(index), 0, keepdims=False)
            lines.append(line.reshape(rows, nv, cols).transpose(1, 0, 2))
        pieces = jnp.concatenate(lines)
        summed = lax.psum_scatter(pieces, ("ctx", "vocab"), scatter_dimension=0, tiled=False)
        along = gather_x(summed)
        along = jnp.concatenate([along, core.swap(along, 1)])
        return along.reshape(nc * rows, cols)

    def final_move(value):
        pairs = []
        ratio = nv // nc
        for i in range(nc):
            for j in range(nv):
                pairs.append((i * nv + j, (j // ratio) * nv + i * ratio + j % ratio))
        return lax.ppermute(value, ("ctx", "vocab"), pairs)

    def back(proj_grad, weight):
        def product(place):
            picked = [
                cut(proj_grad, relative_place((p * vb + place) // 2) * rows, rows, 0)
                for p in range(va)
            ]
            weight_half = cut(weight, (place % 2) * cols, cols, 0)
            return contract_last(jnp.concatenate(picked), weight_half)

        sends = [dim_b.swap(product(b ^ r).astype(BF16), r) for r in range(1, vb)]
        kept = product(b)
        for got in sends:
            kept = kept + got.astype(F32)
        kept = kept.astype(BF16).reshape(va, rows, cols)
        return final_move(halving_scatter(kept, dim_a).astype(BF16)).astype(F32)

    normed_h, normed_e, halves, gathered, row_scales = [], [], [], [], []
    for part in range(PARTS):
        nh, ne = inputs(part)
        projected, part_h, part_e = project(nh, ne)
        rows_all, row_scale = spread(projected)
        normed_h.append(nh)
        normed_e.append(ne)
        halves.append((part_h, part_e))
        gathered.append(rows_all)
        row_scales.append(row_scale)

    logit_grads, scaled_dots = [], []
    mean_loss = F32(0.0)
    for part in range(PARTS):
        scaled_grad, scaled_dot, loss = cross_entropy(part, gathered[part], row_scales[part])
        logit_grads.append(scaled_grad)
        scaled_dots.append(scaled_dot)
        mean_loss = mean_loss + loss
    mean_loss = mean_loss / token_total

    proj_grads, hidden_backs, embed_backs, dots = [], [], [], []
    grad_final_gain = jnp.zeros((cols,), F32)
    for part in range(PARTS):
        scaled = collect(logit_grads[part]).astype(F32)
        projected = cut(gathered[part], slot * cols, cols, 1).astype(F32) / final_gain
        grad_final_gain = grad_final_gain + jnp.sum(scaled * projected, axis=0)
        coefficient = row_scales[part] * row_scales[part] * scaled_dots[part] / width
        proj_grad = (scaled * final_gain - projected * coefficient[:, None]).astype(BF16)
        proj_grads.append(proj_grad)
        wide = proj_grad.astype(F32)
        part_h, part_e = halves[part]
        sums = jnp.stack([jnp.sum(wide * part_h, axis=-1), jnp.sum(wide * part_e, axis=-1)])
        sums = absolute(sums)
        sums = jnp.broadcast_to(sums.transpose(1, 0, 2)[:, None], (nc, nv, 2, rows))
        sums = lax.all_to_all(
            sums.reshape(nc * nv, 2, rows), ("ctx", "vocab"), 0, 0, tiled=True
        )
        dots.append(jnp.sum(sums, axis=0))
        hidden_backs.append(back(proj_grad, proj_hidden))
        embed_backs.append(back(proj_grad, proj_embed))

    rows_all = jnp.concatenate(gathered)
    grad_head = contract_first(jnp.concatenate(logit_grads), rows_all).astype(BF16)
    proj_grad = jnp.concatenate(proj_grads)
    grad_proj_hidden = contract_first(jnp.concatenate(normed_h), proj_grad).astype(BF16)
    grad_proj_embed = contract_first(jnp.concatenate(normed_e), proj_grad).astype(BF16)

    def finish(backs, wide, gain, kind):
        back_all = jnp.concatenate(backs)
        scale = scales[kind][:, None]
        dot_all = jnp.concatenate([pair[kind] for pair in dots])[:, None]
        source = cut(wide, slot * cols, cols, 1).astype(F32)
        gain_piece = cut(gain, slot * cols, cols, 0)
        grad = scale * (back_all * gain_piece) - source * (scale * scale) * (dot_all / width)
        return grad.astype(BF16), jnp.sum(back_all * source * scale, axis=0)

    grad_hidden, gain_h = finish(hidden_backs, hidden_state, gain_hidden, 0)
    grad_embed, gain_e = finish(embed_backs, embedded_next, gain_embed, 1)
    gain_h, gain_e = lax.psum((gain_h, gain_e), "ctx")
    return (
        mean_loss,
        grad_hidden,
        grad_embed,
        gain_h,
        gain_e,
        grad_proj_hidden,
        grad_proj_embed,
        grad_final_gain,
        grad_head,
    )


def solution(mesh):
    in_specs = (
        P("ctx", None),
        P("ctx", None),
        P(),
        P(),
        P("ctx", "vocab"),
        P("ctx", "vocab"),
        P("vocab"),
        P(("ctx", "vocab"), None),
        P(),
        P(),
    )
    out_specs = (
        P(),
        P("ctx", "vocab"),
        P("ctx", "vocab"),
        P("vocab"),
        P("vocab"),
        P("ctx", "vocab"),
        P("ctx", "vocab"),
        P("vocab"),
        P(("ctx", "vocab"), None),
    )
    return jax.shard_map(local, mesh=mesh, in_specs=in_specs, out_specs=out_specs, check_vma=False)
```

```python
import jax
import jax.numpy as jnp
from jax import lax
from jax.sharding import PartitionSpec as P

EPSILON = 1e-06
PARTS = 2
F32 = jnp.float32
BF16 = jnp.bfloat16


class Dim:
    def __init__(self, axis, size, n, stride):
        self.axis, self.size, self.n, self.stride = axis, size, n, stride

    def place(self):
        return (lax.axis_index(self.axis) // self.stride) % self.n

    def move(self, value, target):
        pairs = []
        for index in range(self.size):
            here = (index // self.stride) % self.n
            there = target(here)
            if there is not None and 0 <= there < self.n:
                pairs.append((index, index + (there - here) * self.stride))
        return lax.ppermute(value, self.axis, pairs)

    def swap(self, value, bit):
        return self.move(value, lambda here: here ^ bit)

    def turn(self, value, by):
        return self.move(value, lambda here: (here + by) % self.n)


def halving_scatter(chunks, dim):
    here = dim.place()
    held = {
        offset: lax.dynamic_index_in_dim(chunks, here ^ offset, 0, keepdims=False)
        for offset in range(dim.n)
    }
    bit = 1
    while bit < dim.n:
        send = jnp.stack([held[offset] for offset in range(dim.n) if offset in held and offset & bit])
        got = dim.swap(send, bit)
        keep = [offset for offset in sorted(held) if not offset & bit]
        held = {
            offset: (held[offset].astype(F32) + got[index].astype(F32))
            for index, offset in enumerate(keep)
        }
        bit *= 2
        if bit < dim.n:
            held = {offset: piece.astype(BF16) for offset, piece in held.items()}
    return held[0]


def sum_everywhere(value):
    axes = ("ctx", "vocab")
    count = lax.axis_size("ctx") * lax.axis_size("vocab")
    copies = jnp.broadcast_to(value[None], (count,) + value.shape)
    return jnp.sum(lax.all_to_all(copies, axes, 0, 0, tiled=True), axis=0)


def contract_first(left, right):
    return lax.dot_general(left, right, (((0,), (0,)), ((), ())), preferred_element_type=F32)


def contract_last(left, right):
    return lax.dot_general(left, right, (((1,), (1,)), ((), ())), preferred_element_type=F32)


def dot(left, right):
    return jnp.dot(left, right, preferred_element_type=F32)


def cut(array, start, width, axis):
    return lax.dynamic_slice_in_dim(array, start, width, axis)


def local(
    hidden_state,
    embedded_next,
    gain_hidden,
    gain_embed,
    proj_hidden,
    proj_embed,
    final_gain,
    head,
    targets,
    loss_mask,
):
    nc, nv = lax.axis_size("ctx"), lax.axis_size("vocab")
    nx, va = nc // 2, 4
    vb = nv // va
    core = Dim("ctx", nc, 2, 1)
    dim_x = Dim("ctx", nc, nx, 2)
    dim_b = Dim("vocab", nv, vb, 1)
    dim_a = Dim("vocab", nv, va, vb)
    own, slot = lax.axis_index("ctx"), lax.axis_index("vocab")
    x, c, b = own // 2, own % 2, slot % vb

    width = hidden_state.shape[1]
    block = hidden_state.shape[0]
    token_total = targets.shape[0]
    feat, cols = proj_hidden.shape
    rows = block // PARTS
    part_rows = nc * rows
    vocab_local = head.shape[0]

    def relative_place(block_index):
        return (c ^ (block_index % 2)) * nx + (x - block_index // 2) % nx

    def block_at(place):
        return ((x - place % nx) % nx) * 2 + (c ^ (place // nx))

    order = jnp.stack([relative_place(jnp.int32(i)) for i in range(nc)])
    to_absolute = (order[:, None] == jnp.arange(nc, dtype=jnp.int32)[None, :])[:, :, None, None]

    def absolute(value):
        value = value.reshape(value.shape[:-1] + (PARTS, nc, rows))
        value = jnp.swapaxes(value, -3, -2)[..., None, :, :, :]
        return jnp.sum(jnp.where(to_absolute, value, 0), axis=-3).reshape(
            value.shape[:-4] + (nc, block)
        )

    def relative(value):
        value = value.reshape(value.shape[:-1] + (PARTS, rows))[..., :, None, :, :]
        value = jnp.sum(jnp.where(to_absolute, value, 0), axis=-4)
        return jnp.swapaxes(value, -3, -2).reshape(value.shape[:-3] + (token_total,))

    def by_part(pieces):
        return jnp.concatenate(
            [piece[part * rows : (part + 1) * rows] for part in range(PARTS) for piece in pieces]
        )

    def gather_x(value):
        return jnp.stack([value] + [dim_x.turn(value, r) for r in range(1, nx)])

    def x_sends(wide):
        return [cut(wide, ((x + r) % nx) * 2 * feat, 2 * feat, 1) for r in range(1, nx)]

    hidden_sends, embed_sends = x_sends(hidden_state), x_sends(embedded_next)
    hidden_sends, embed_sends, hidden_state, embedded_next = lax.optimization_barrier(
        (hidden_sends, embed_sends, hidden_state, embedded_next)
    )
    hidden_x = [dim_x.turn(send, r + 1) for r, send in enumerate(hidden_sends)]
    embed_x = [dim_x.turn(send, r + 1) for r, send in enumerate(embed_sends)]

    hidden_wide, embed_wide = hidden_state.astype(F32), embedded_next.astype(F32)
    scales = lax.rsqrt(
        jnp.stack(
            [jnp.mean(hidden_wide * hidden_wide, axis=-1), jnp.mean(embed_wide * embed_wide, axis=-1)]
        )
        + EPSILON
    )
    scales_x = gather_x(scales)
    scales_all = jnp.concatenate([scales_x, core.swap(scales_x, 1)])

    def normed_inputs(wide, from_x, gain, kind):
        pieces = [cut(wide, x * 2 * feat, 2 * feat, 1)] + from_x
        mine = [cut(piece, c * feat, feat, 1) for piece in pieces]
        theirs = [core.swap(cut(piece, (1 - c) * feat, feat, 1), 1) for piece in pieces]
        raw = by_part(mine + theirs).astype(F32)
        scale = by_part([scales_all[place, kind][:, None] for place in range(nc)])
        return (raw * scale * cut(gain, own * feat, feat, 0)).astype(BF16)

    normed_h = normed_inputs(hidden_state, hidden_x, gain_hidden, 0)
    normed_e = normed_inputs(embedded_next, embed_x, gain_embed, 1)

    half_h, half_e = dot(normed_h, proj_hidden), dot(normed_e, proj_embed)
    total = (half_h + half_e).reshape(PARTS, 2, nx, rows, cols)
    mine = total[:, 0] + core.swap(total[:, 1].astype(BF16), 1).astype(F32)
    projected = mine[:, 0]
    for r in range(1, nx):
        projected = projected + dim_x.turn(mine[:, r].astype(BF16), -r).astype(F32)
    projected = projected.reshape(block, cols)

    pieces = lax.all_gather((projected * final_gain).astype(BF16), ("ctx", "vocab"))
    squares = jnp.sum(projected * projected, axis=-1)
    squares = lax.all_to_all(
        jnp.broadcast_to(squares, (nc * nv, block)), ("ctx", "vocab"), 0, 0, tiled=True
    )
    squares = jnp.sum(squares.reshape(nc, nv, block), axis=1)
    row_scale = relative(lax.rsqrt(squares / width + EPSILON))
    pieces = pieces.reshape(nc, nv, block, cols)
    gathered = by_part(
        [
            lax.dynamic_index_in_dim(pieces, block_at(place), 0, keepdims=False)
            .transpose(1, 0, 2)
            .reshape(block, width)
            for place in range(nc)
        ]
    )

    vocab_ids = (own * nv + slot) * vocab_local + lax.iota(jnp.int32, vocab_local)
    logits = contract_last(gathered, head) * row_scale[:, None]
    target = relative(targets.reshape(nc, block))
    mask_weight = loss_mask.astype(F32).reshape(nc, block)
    mask = relative(mask_weight)
    is_target = target[:, None] == vocab_ids[None, :]
    power = jnp.exp(logits)
    sums = jnp.stack(
        [
            jnp.sum(power, axis=-1),
            jnp.sum(power * (logits * F32(1.0 / 256.0)), axis=-1),
            jnp.sum(jnp.where(is_target, logits, F32(0.0)), axis=-1),
        ]
    )
    sums = sum_everywhere(absolute(sums))
    exp_total, weighted, target_logit = sums[0], sums[1], sums[2]
    log_total = jnp.log(exp_total)
    mean_loss = jnp.sum(mask_weight * (log_total - target_logit)) / token_total
    scaled_dot = mask * relative(weighted / exp_total * F32(256.0) - target_logit)
    probs = jnp.exp(logits - relative(log_total)[:, None])
    scaled_grad = ((mask * row_scale)[:, None] * (probs - is_target.astype(F32))).astype(BF16)
    coefficient = row_scale * row_scale * scaled_dot / width

    def column_chunk(value, place):
        return jnp.stack([cut(value, (p * vb + place) * cols, cols, 1) for p in range(va)])

    def collect(part_grad):
        partial = dot(part_grad, head).astype(BF16)
        mine, theirs = partial[: nx * rows], partial[nx * rows :]
        mine = (mine.astype(F32) + core.swap(theirs, 1).astype(F32)).astype(BF16)
        mine = mine.reshape(nx, rows, width)
        summed = mine[0].astype(F32)
        for r in range(1, nx):
            summed = summed + dim_x.turn(mine[r], -r).astype(F32)
        summed = summed.astype(BF16)
        kept = column_chunk(summed, b).astype(F32)
        for r in range(1, vb):
            kept = kept + dim_b.turn(column_chunk(summed, (b + r) % vb), r).astype(F32)
        summed = halving_scatter(kept.astype(BF16), dim_a).astype(BF16)
        along = gather_x(summed)
        along = jnp.concatenate([along, core.swap(along, 1)])
        return along.reshape(part_rows, cols)

    def final_move(value):
        pairs = []
        ratio = nv // nc
        for i in range(nc):
            for j in range(nv):
                pairs.append((i * nv + j, (j // ratio) * nv + i * ratio + j % ratio))
        return lax.ppermute(value, ("ctx", "vocab"), pairs)

    def back(part_grad):
        def products(place):
            picked = jnp.concatenate(
                [
                    cut(part_grad, relative_place((p * vb + place) // 2) * rows, rows, 0)
                    for p in range(va)
                ]
            )
            return [
                contract_last(picked, cut(weight, (place % 2) * cols, cols, 0)).reshape(
                    va, rows, cols
                )
                for weight in (proj_hidden, proj_embed)
            ]

        sends = [
            dim_b.swap(jnp.concatenate(products(b ^ r), axis=1).astype(BF16), r)
            for r in range(1, vb)
        ]
        kept = jnp.concatenate(products(b), axis=1)
        for got in sends:
            kept = kept + got.astype(F32)
        moved = final_move(halving_scatter(kept.astype(BF16), dim_a).astype(BF16))
        return moved.astype(F32)

    grad_final_gain = jnp.zeros((cols,), F32)
    proj_grads, backs = [], []
    for part in range(PARTS):
        span = slice(part * part_rows, (part + 1) * part_rows)
        scaled = collect(scaled_grad[span]).astype(F32)
        plain = cut(gathered[span], slot * cols, cols, 1).astype(F32) / final_gain
        grad_final_gain = grad_final_gain + jnp.sum(scaled * plain, axis=0)
        part_grad = (scaled * final_gain - plain * coefficient[span][:, None]).astype(BF16)
        proj_grads.append(part_grad)
        backs.append(back(part_grad))

    grad_head = contract_first(scaled_grad, gathered).astype(BF16)
    proj_grad = jnp.concatenate(proj_grads)
    wide_h, wide_e = contract_first(normed_h, proj_grad), contract_first(normed_e, proj_grad)
    grad_proj_hidden, grad_proj_embed = wide_h.astype(BF16), wide_e.astype(BF16)

    wide = proj_grad.astype(F32)
    dots = absolute(jnp.stack([jnp.sum(wide * half_h, axis=-1), jnp.sum(wide * half_e, axis=-1)]))
    dots = jnp.broadcast_to(dots.transpose(1, 0, 2)[:, None], (nc, nv, 2, block))
    gains = jnp.stack(
        [
            jnp.sum(wide_h * proj_hidden.astype(F32), axis=1),
            jnp.sum(wide_e * proj_embed.astype(F32), axis=1),
        ]
    )
    ratio = nv // nc
    gains = gains.reshape(2, ratio, cols).transpose(1, 0, 2)[None]
    holder = jnp.arange(nc, dtype=jnp.int32)[:, None, None, None] == own
    gains = jnp.where(holder, gains, F32(0.0)).reshape(nv, 2, cols)
    gains = jnp.broadcast_to(gains[None], (nc, nv, 2, cols))
    ends = jnp.concatenate([dots, gains], axis=-1).reshape(nc * nv, 2, block + cols)
    ends = jnp.sum(lax.all_to_all(ends, ("ctx", "vocab"), 0, 0, tiled=True), axis=0)

    def finish(kind, source, gain):
        back_all = jnp.concatenate([moved[kind * rows : (kind + 1) * rows] for moved in backs])
        scale = scales[kind][:, None]
        dot_all = ends[kind, :block][:, None]
        source = cut(source, slot * cols, cols, 1).astype(F32)
        gain = cut(gain, slot * cols, cols, 0)
        grad = scale * (back_all * gain) - source * (scale * scale) * (dot_all / width)
        return grad.astype(BF16), ends[kind, block:] / gain

    grad_hidden, grad_gain_hidden = finish(0, hidden_state, gain_hidden)
    grad_embed, grad_gain_embed = finish(1, embedded_next, gain_embed)
    return (
        mean_loss,
        grad_hidden,
        grad_embed,
        grad_gain_hidden,
        grad_gain_embed,
        grad_proj_hidden,
        grad_proj_embed,
        grad_final_gain,
        grad_head,
    )


def solution(mesh):
    in_specs = (
        P("ctx", None),
        P("ctx", None),
        P(),
        P(),
        P("ctx", "vocab"),
        P("ctx", "vocab"),
        P("vocab"),
        P(("ctx", "vocab"), None),
        P(),
        P(),
    )
    out_specs = (
        P(),
        P("ctx", "vocab"),
        P("ctx", "vocab"),
        P("vocab"),
        P("vocab"),
        P("ctx", "vocab"),
        P("ctx", "vocab"),
        P("vocab"),
        P(("ctx", "vocab"), None),
    )
    return jax.shard_map(local, mesh=mesh, in_specs=in_specs, out_specs=out_specs, check_vma=False)
```

```python
import jax
import jax.numpy as jnp
from jax import lax
from jax.experimental import pallas as pl
from jax.experimental.pallas import tpu as pltpu
from jax.sharding import PartitionSpec as P

EPSILON = 1e-06
PARTS = 2
F32 = jnp.float32
BF16 = jnp.bfloat16


class Dim:
    def __init__(self, axis, size, n, stride):
        self.axis, self.size, self.n, self.stride = axis, size, n, stride

    def place(self):
        return (lax.axis_index(self.axis) // self.stride) % self.n

    def move(self, value, target):
        pairs = []
        for index in range(self.size):
            here = (index // self.stride) % self.n
            there = target(here)
            if there is not None and 0 <= there < self.n:
                pairs.append((index, index + (there - here) * self.stride))
        return lax.ppermute(value, self.axis, pairs)

    def swap(self, value, bit):
        return self.move(value, lambda here: here ^ bit)

    def turn(self, value, by):
        return self.move(value, lambda here: (here + by) % self.n)


def halving_scatter(chunks, dim):
    here = dim.place()
    held = {
        offset: lax.dynamic_index_in_dim(chunks, here ^ offset, 0, keepdims=False)
        for offset in range(dim.n)
    }
    bit = 1
    while bit < dim.n:
        send = jnp.stack([held[offset] for offset in range(dim.n) if offset in held and offset & bit])
        got = dim.swap(send, bit)
        keep = [offset for offset in sorted(held) if not offset & bit]
        held = {
            offset: (held[offset].astype(F32) + got[index].astype(F32))
            for index, offset in enumerate(keep)
        }
        bit *= 2
        if bit < dim.n:
            held = {offset: piece.astype(BF16) for offset, piece in held.items()}
    return held[0]


def sum_everywhere(value):
    axes = ("ctx", "vocab")
    count = lax.axis_size("ctx") * lax.axis_size("vocab")
    copies = jnp.broadcast_to(value[None], (count,) + value.shape)
    return jnp.sum(lax.all_to_all(copies, axes, 0, 0, tiled=True), axis=0)


def contract_first(left, right):
    return lax.dot_general(left, right, (((0,), (0,)), ((), ())), preferred_element_type=F32)


def contract_last(left, right):
    return lax.dot_general(left, right, (((1,), (1,)), ((), ())), preferred_element_type=F32)


def whole_block(shape):
    return pl.BlockSpec(shape, lambda *step: (0,) * len(shape), pipeline_mode=pl.Buffered(1))


def kernel_call(body, grid, in_specs, out_specs, out_shape, flops, moved, exps=0):
    return pl.pallas_call(
        body,
        grid=grid,
        in_specs=in_specs,
        out_specs=out_specs,
        out_shape=out_shape,
        compiler_params=pltpu.CompilerParams(vmem_limit_bytes=48 * 1024 * 1024),
        cost_estimate=pl.CostEstimate(flops=flops, bytes_accessed=moved, transcendentals=exps),
    )


def logits_with_sums(rows_all, head, row_scale, target):
    tokens, width = rows_all.shape
    entries = head.shape[0]
    tile = 256

    def body(rows_ref, head_ref, scale_ref, target_ref, logits_ref, sums_ref):
        step = pl.program_id(0)
        logits = contract_last(rows_ref[...], head_ref[...]) * scale_ref[...]
        logits_ref[...] = logits
        power = jnp.exp(logits)
        ids = lax.broadcasted_iota(jnp.int32, logits.shape, 1) + step * tile
        chosen = jnp.where(ids == target_ref[...], logits, 0.0)
        terms = (power, power * (logits * F32(1.0 / 256.0)), chosen)

        @pl.when(step == 0)
        def _():
            sums_ref[...] = jnp.zeros_like(sums_ref)

        for index, term in enumerate(terms):
            folded = term[:, :128]
            for lane in range(128, tile, 128):
                folded = folded + term[:, lane : lane + 128]
            sums_ref[index] += folded

    return kernel_call(
        body,
        (entries // tile,),
        [
            whole_block((tokens, width)),
            pl.BlockSpec((tile, width), lambda step: (step, 0)),
            whole_block((tokens, 1)),
            whole_block((tokens, 1)),
        ],
        [
            pl.BlockSpec((tokens, tile), lambda step: (0, step)),
            pl.BlockSpec((3, tokens, 128), lambda step: (0, 0, 0)),
        ],
        [
            jax.ShapeDtypeStruct((tokens, entries), F32),
            jax.ShapeDtypeStruct((3, tokens, 128), F32),
        ],
        2 * tokens * width * entries,
        2 * entries * width + 2 * tokens * width + 4 * tokens * entries,
        tokens * entries,
    )(rows_all, head, row_scale[:, None], target[:, None])


def times_head(grad, head):
    tokens, entries = grad.shape
    width = head.shape[1]
    tile = 512

    def body(grad_ref, head_ref, out_ref):
        out_ref[...] = dot(grad_ref[...], head_ref[...]).astype(BF16)

    return kernel_call(
        body,
        (width // tile,),
        [whole_block((tokens, entries)), pl.BlockSpec((entries, tile), lambda step: (0, step))],
        pl.BlockSpec((tokens, tile), lambda step: (0, step)),
        jax.ShapeDtypeStruct((tokens, width), BF16),
        2 * tokens * width * entries,
        2 * entries * width + 2 * tokens * width + 2 * tokens * entries,
    )(grad, head)


def head_gradient(grads, rows_all, after):
    tokens, entries = grads[0].shape
    width = rows_all[0].shape[1]
    tile, chunk = 256, 1024
    parts = len(grads)

    def body(*refs):
        grad_refs, row_refs, out_ref = refs[:parts], refs[parts : 2 * parts], refs[-1]
        for start in range(0, width, chunk):
            total = None
            for grad_ref, row_ref in zip(grad_refs, row_refs):
                term = contract_first(grad_ref[...], row_ref[:, start : start + chunk])
                total = term if total is None else total + term
            out_ref[:, start : start + chunk] = total.astype(BF16)

    return kernel_call(
        body,
        (entries // tile,),
        [pl.BlockSpec((tokens, tile), lambda step: (0, step))] * parts
        + [whole_block((tokens, width))] * parts
        + [pl.BlockSpec(memory_space=pl.ANY)] * len(after),
        pl.BlockSpec((tile, width), lambda step: (step, 0)),
        jax.ShapeDtypeStruct((entries, width), BF16),
        2 * parts * tokens * width * entries,
        2 * entries * width + 2 * parts * tokens * (width + entries),
    )(*grads, *rows_all, *after)


def weight_gradient(normed, proj_grad, weight):
    tokens, feat = normed.shape
    cols = proj_grad.shape[1]
    tile = 256 if feat % 256 == 0 else 128

    def body(normed_ref, grad_ref, weight_ref, out_ref, sum_ref):
        grad = contract_first(normed_ref[...], grad_ref[...])
        out_ref[...] = grad.astype(BF16)
        total = jnp.sum(grad * weight_ref[...].astype(F32), axis=1, keepdims=True)
        sum_ref[...] = jnp.broadcast_to(total, sum_ref.shape)

    out, sums = kernel_call(
        body,
        (feat // tile,),
        [
            pl.BlockSpec((tokens, tile), lambda step: (0, step)),
            whole_block((tokens, cols)),
            pl.BlockSpec((tile, cols), lambda step: (step, 0)),
        ],
        [
            pl.BlockSpec((tile, cols), lambda step: (step, 0)),
            pl.BlockSpec((tile, 128), lambda step: (step, 0)),
        ],
        [
            jax.ShapeDtypeStruct((feat, cols), BF16),
            jax.ShapeDtypeStruct((feat, 128), F32),
        ],
        2 * tokens * feat * cols,
        4 * feat * cols + 2 * tokens * (feat + cols),
    )(normed, proj_grad, weight)
    return out, sums[:, 0]


def dot(left, right):
    return jnp.dot(left, right, preferred_element_type=F32)


def cut(array, start, width, axis):
    return lax.dynamic_slice_in_dim(array, start, width, axis)


def local(
    hidden_state,
    embedded_next,
    gain_hidden,
    gain_embed,
    proj_hidden,
    proj_embed,
    final_gain,
    head,
    targets,
    loss_mask,
):
    nc, nv = lax.axis_size("ctx"), lax.axis_size("vocab")
    nx, va = nc // 2, 4
    vb = nv // va
    core = Dim("ctx", nc, 2, 1)
    dim_x = Dim("ctx", nc, nx, 2)
    dim_b = Dim("vocab", nv, vb, 1)
    dim_a = Dim("vocab", nv, va, vb)
    own, slot = lax.axis_index("ctx"), lax.axis_index("vocab")
    x, c, b = own // 2, own % 2, slot % vb

    width = hidden_state.shape[1]
    block = hidden_state.shape[0]
    token_total = targets.shape[0]
    feat, cols = proj_hidden.shape
    rows = block // PARTS
    part_rows = nc * rows
    vocab_local = head.shape[0]

    def relative_place(block_index):
        return (c ^ (block_index % 2)) * nx + (x - block_index // 2) % nx

    def block_at(place):
        return ((x - place % nx) % nx) * 2 + (c ^ (place // nx))

    order = jnp.stack([relative_place(jnp.int32(i)) for i in range(nc)])
    to_absolute = (order[:, None] == jnp.arange(nc, dtype=jnp.int32)[None, :])[:, :, None, None]

    def absolute(value):
        value = value.reshape(value.shape[:-1] + (PARTS, nc, rows))
        value = jnp.swapaxes(value, -3, -2)[..., None, :, :, :]
        return jnp.sum(jnp.where(to_absolute, value, 0), axis=-3).reshape(
            value.shape[:-4] + (nc, block)
        )

    def relative(value):
        value = value.reshape(value.shape[:-1] + (PARTS, rows))[..., :, None, :, :]
        value = jnp.sum(jnp.where(to_absolute, value, 0), axis=-4)
        return jnp.swapaxes(value, -3, -2).reshape(value.shape[:-3] + (token_total,))

    def absolute_part(value):
        value = value.reshape(value.shape[0], nc, rows, value.shape[-1])[:, None]
        return jnp.sum(jnp.where(to_absolute[..., 0, :, None], value, 0), axis=2)

    def relative_part(value):
        return jnp.sum(jnp.where(to_absolute[..., 0], value[:, None], 0), axis=0).reshape(part_rows)

    places = [(rc, rx) for rc in range(2) for rx in range(nx)]

    def send(value, rc, rx):
        pairs = []
        for i in range(nc):
            pairs.append((i, ((i // 2 + rx) % nx) * 2 + ((i % 2) ^ rc)))
        return lax.ppermute(value, "ctx", pairs)

    def scale_of(wide):
        wide = wide.astype(F32)
        return lax.rsqrt(jnp.mean(wide * wide, axis=-1, keepdims=True) + EPSILON)

    def normed_blocks(wide, scale, gain):
        def piece(rc, rx):
            start = (((x + rx) % nx) * 2 + (c ^ rc)) * feat
            value = cut(wide, start, feat, 1).astype(F32)
            return (value * scale * cut(gain, start, feat, 0)).astype(BF16)

        far = {(rc, rx): send(piece(rc, rx), rc, rx) for rx in range(1, nx) for rc in range(2)}
        far[1, 0] = send(piece(1, 0), 1, 0)
        far[0, 0] = piece(0, 0)
        return [far[place] for place in places]

    hidden_scale, embed_scale = scale_of(hidden_state), scale_of(embedded_next)
    blocks_h = normed_blocks(hidden_state, hidden_scale, gain_hidden)
    blocks_e = normed_blocks(embedded_next, embed_scale, gain_embed)

    halves_h = [dot(piece, proj_hidden) for piece in blocks_h]
    halves_e = [dot(piece, proj_embed) for piece in blocks_e]
    projected = halves_h[0] + halves_e[0]
    for index, (rc, rx) in enumerate(places[1:], 1):
        term = (halves_h[index] + halves_e[index]).astype(BF16)
        projected = projected + send(term, rc, (nx - rx) % nx).astype(F32)

    piece = (projected * final_gain).astype(BF16)
    squares = jnp.sum(projected * projected, axis=-1)
    squares = lax.all_to_all(
        jnp.broadcast_to(squares, (nc * nv, block)), ("ctx", "vocab"), 0, 0, tiled=True
    )
    squares = jnp.sum(squares.reshape(nc, nv, block), axis=1)
    row_scales = relative(lax.rsqrt(squares / width + EPSILON))
    target_local = relative(targets.reshape(nc, block)) - (own * nv + slot) * vocab_local
    mask_weight = loss_mask.astype(F32).reshape(nc, block)
    mask = relative(mask_weight)
    gathered, logit_list, sum_list = [], [], []
    for part in range(PARTS):
        span = slice(part * part_rows, (part + 1) * part_rows)
        pieces = lax.all_gather(piece[part * rows : (part + 1) * rows], ("ctx", "vocab"))
        pieces = pieces.reshape(nc, nv, rows, cols)
        gathered.append(
            jnp.concatenate(
                [
                    lax.dynamic_index_in_dim(pieces, block_at(place), 0, keepdims=False)
                    .transpose(1, 0, 2)
                    .reshape(rows, width)
                    for place in range(nc)
                ]
            )
        )
        logits, sums = logits_with_sums(gathered[part], head, row_scales[span], target_local[span])
        logit_list.append(logits)
        sum_list.append(sum_everywhere(jnp.sum(absolute_part(sums), axis=-1)))

    mean_loss = F32(0.0)
    logit_grads, coefficients = [], []
    vocab_ids = lax.iota(jnp.int32, vocab_local)[None, :]
    for part in range(PARTS):
        span = slice(part * part_rows, (part + 1) * part_rows)
        exp_total, weighted, target_logit = sum_list[part]
        log_total = jnp.log(exp_total)
        part_mask = mask_weight[:, part * rows : (part + 1) * rows]
        mean_loss = mean_loss + jnp.sum(part_mask * (log_total - target_logit))
        scaled_dot = mask[span] * relative_part(weighted / exp_total * F32(256.0) - target_logit)
        row_scale = row_scales[span]
        probs = jnp.exp(logit_list[part] - relative_part(log_total)[:, None])
        is_target = target_local[span][:, None] == vocab_ids
        logit_grads.append(
            ((mask[span] * row_scale)[:, None] * (probs - is_target.astype(F32))).astype(BF16)
        )
        coefficients.append(row_scale * row_scale * scaled_dot / width)
    mean_loss = mean_loss / token_total

    def column_chunk(value, place):
        return jnp.stack([cut(value, (p * vb + place) * cols, cols, 1) for p in range(va)])

    def core_sum(partial):
        mine, theirs = partial[: nx * rows], partial[nx * rows :]
        return (mine.astype(F32) + core.swap(theirs, 1).astype(F32)).astype(BF16)

    def collect(mine):
        mine = mine.reshape(nx, rows, width)
        summed = mine[0].astype(F32)
        for r in range(1, nx):
            summed = summed + dim_x.turn(mine[r], -r).astype(F32)
        summed = summed.astype(BF16)
        kept = column_chunk(summed, b).astype(F32)
        for r in range(1, vb):
            kept = kept + dim_b.turn(column_chunk(summed, (b + r) % vb), r).astype(F32)
        summed = halving_scatter(kept.astype(BF16), dim_a).astype(BF16)
        return jnp.concatenate([summed] + [send(summed, rc, rx) for rc, rx in places[1:]])

    def final_move(value):
        pairs = []
        ratio = nv // nc
        for i in range(nc):
            for j in range(nv):
                pairs.append((i * nv + j, (j // ratio) * nv + i * ratio + j % ratio))
        return lax.ppermute(value, ("ctx", "vocab"), pairs)

    def back(part_grad):
        def products(place):
            picked = jnp.concatenate(
                [
                    cut(part_grad, relative_place((p * vb + place) // 2) * rows, rows, 0)
                    for p in range(va)
                ]
            )
            return [
                contract_last(picked, cut(weight, (place % 2) * cols, cols, 0)).reshape(
                    va, rows, cols
                )
                for weight in (proj_hidden, proj_embed)
            ]

        sends = [
            dim_b.swap(jnp.concatenate(products(b ^ r), axis=1).astype(BF16), r)
            for r in range(1, vb)
        ]
        kept = jnp.concatenate(products(b), axis=1)
        for got in sends:
            kept = kept + got.astype(F32)
        moved = final_move(halving_scatter(kept.astype(BF16), dim_a).astype(BF16))
        return moved.astype(F32)

    core_sums = [core_sum(times_head(part_grad, head)) for part_grad in logit_grads]
    grad_head = head_gradient(logit_grads, gathered, core_sums)
    grad_final_gain = jnp.zeros((cols,), F32)
    proj_grads, backs = [], []
    for part in range(PARTS):
        scaled = collect(core_sums[part]).astype(F32)
        plain = cut(gathered[part], slot * cols, cols, 1).astype(F32) / final_gain
        grad_final_gain = grad_final_gain + jnp.sum(scaled * plain, axis=0)
        part_grad = scaled * final_gain - plain * coefficients[part][:, None]
        proj_grads.append(part_grad.astype(BF16))
        backs.append(back(proj_grads[part]))

    proj_grad = jnp.stack([grad.reshape(nc, rows, cols) for grad in proj_grads], axis=1)
    grad_proj_hidden, gain_h = weight_gradient(
        jnp.concatenate(blocks_h), proj_grad.reshape(token_total, cols), proj_hidden
    )
    grad_proj_embed, gain_e = weight_gradient(
        jnp.concatenate(blocks_e), proj_grad.reshape(token_total, cols), proj_embed
    )

    wide = proj_grad.astype(F32).reshape(nc, block, cols)
    dots = jnp.stack(
        [jnp.sum(wide * jnp.stack(halves), axis=-1) for halves in (halves_h, halves_e)]
    )
    dots = jnp.sum(jnp.where(to_absolute[..., 0], dots[:, None], 0), axis=2)
    dots = jnp.broadcast_to(dots.transpose(1, 0, 2)[:, None], (nc, nv, 2, block))
    gains = jnp.stack([gain_h, gain_e])
    ratio = nv // nc
    gains = gains.reshape(2, ratio, cols).transpose(1, 0, 2)[None]
    holder = jnp.arange(nc, dtype=jnp.int32)[:, None, None, None] == own
    gains = jnp.where(holder, gains, F32(0.0)).reshape(nv, 2, cols)
    gains = jnp.broadcast_to(gains[None], (nc, nv, 2, cols))
    ends = jnp.concatenate([dots, gains], axis=-1).reshape(nc * nv, 2, block + cols)
    ends = jnp.sum(lax.all_to_all(ends, ("ctx", "vocab"), 0, 0, tiled=True), axis=0)

    def finish(kind, source, gain):
        back_all = jnp.concatenate([moved[kind * rows : (kind + 1) * rows] for moved in backs])
        scale = (hidden_scale, embed_scale)[kind]
        dot_all = ends[kind, :block][:, None]
        source = cut(source, slot * cols, cols, 1).astype(F32)
        gain = cut(gain, slot * cols, cols, 0)
        grad = scale * (back_all * gain) - source * (scale * scale) * (dot_all / width)
        return grad.astype(BF16), ends[kind, block:] / gain

    grad_hidden, grad_gain_hidden = finish(0, hidden_state, gain_hidden)
    grad_embed, grad_gain_embed = finish(1, embedded_next, gain_embed)
    return (
        mean_loss,
        grad_hidden,
        grad_embed,
        grad_gain_hidden,
        grad_gain_embed,
        grad_proj_hidden,
        grad_proj_embed,
        grad_final_gain,
        grad_head,
    )


def solution(mesh):
    in_specs = (
        P("ctx", None),
        P("ctx", None),
        P(),
        P(),
        P("ctx", "vocab"),
        P("ctx", "vocab"),
        P("vocab"),
        P(("ctx", "vocab"), None),
        P(),
        P(),
    )
    out_specs = (
        P(),
        P("ctx", "vocab"),
        P("ctx", "vocab"),
        P("vocab"),
        P("vocab"),
        P("ctx", "vocab"),
        P("ctx", "vocab"),
        P("vocab"),
        P(("ctx", "vocab"), None),
    )
    return jax.shard_map(local, mesh=mesh, in_specs=in_specs, out_specs=out_specs, check_vma=False)
```

```python
import jax
import jax.numpy as jnp
from jax import lax
from jax.experimental import pallas as pl
from jax.experimental.pallas import tpu as pltpu
from jax.sharding import PartitionSpec as P

EPSILON = 1e-06
TILE = 256
F32 = jnp.float32
BF16 = jnp.bfloat16


class Dim:
    def __init__(self, axis, size, n, stride):
        self.axis, self.size, self.n, self.stride = axis, size, n, stride

    def place(self):
        return (lax.axis_index(self.axis) // self.stride) % self.n

    def move(self, value, target):
        pairs = []
        for index in range(self.size):
            here = (index // self.stride) % self.n
            there = target(here)
            if there is not None and 0 <= there < self.n:
                pairs.append((index, index + (there - here) * self.stride))
        return lax.ppermute(value, self.axis, pairs)

    def swap(self, value, bit):
        return self.move(value, lambda here: here ^ bit)

    def turn(self, value, by):
        return self.move(value, lambda here: (here + by) % self.n)


def exchange_near(chunks, dim):
    here = dim.place()
    pick = [lax.dynamic_index_in_dim(chunks, here ^ bit, 0, keepdims=False) for bit in range(4)]
    got = dim.swap(jnp.stack([pick[1], pick[3]]), 1).astype(F32)
    return pick[0].astype(F32) + got[0], (pick[2].astype(F32) + got[1]).astype(BF16)


def exchange_far(pair, dim):
    near, far = pair
    return (near + dim.swap(far, 2).astype(F32)).astype(BF16)


def sum_everywhere(value):
    axes = ("ctx", "vocab")
    count = lax.axis_size("ctx") * lax.axis_size("vocab")
    copies = jnp.broadcast_to(value[None], (count,) + value.shape)
    return jnp.sum(lax.all_to_all(copies, axes, 0, 0, tiled=True), axis=0)


def contract_first(left, right):
    return lax.dot_general(left, right, (((0,), (0,)), ((), ())), preferred_element_type=F32)


def contract_last(left, right):
    return lax.dot_general(left, right, (((1,), (1,)), ((), ())), preferred_element_type=F32)


def whole_block(shape):
    return pl.BlockSpec(shape, lambda *step: (0,) * len(shape), pipeline_mode=pl.Buffered(1))


def kernel_call(body, grid, in_specs, out_specs, out_shape, flops, moved, exps=0):
    return pl.pallas_call(
        body,
        grid=grid,
        in_specs=in_specs,
        out_specs=out_specs,
        out_shape=out_shape,
        compiler_params=pltpu.CompilerParams(vmem_limit_bytes=48 * 1024 * 1024),
        cost_estimate=pl.CostEstimate(flops=flops, bytes_accessed=moved, transcendentals=exps),
    )


def head_gradient(grad, rows_all, span, after, base=None):
    tokens, entries = grad.shape
    width = rows_all.shape[1]
    chunk = 1024
    begin, end = span
    extra = ([] if base is None else [base]) + list(after)

    def body(grad_ref, rows_ref, *rest):
        out_ref, mark_ref = rest[-2:]
        for start in range(0, width, chunk):
            part = contract_first(grad_ref[...], rows_ref[:, start : start + chunk])
            out_ref[:, start : start + chunk] = part.astype(BF16)
        mark_ref[...] = jnp.zeros_like(mark_ref)

    return pl.pallas_call(
        body,
        grid=(end - begin,),
        in_specs=[
            pl.BlockSpec((tokens, TILE), lambda step: (0, step + begin)),
            whole_block((tokens, width)),
        ]
        + [pl.BlockSpec(memory_space=pl.ANY)] * len(extra),
        out_specs=[
            pl.BlockSpec((TILE, width), lambda step: (step + begin, 0)),
            pl.BlockSpec((8, 128), lambda step: (0, 0)),
        ],
        out_shape=[
            jax.ShapeDtypeStruct((entries, width), BF16),
            jax.ShapeDtypeStruct((8, 128), F32),
        ],
        input_output_aliases={} if base is None else {2: 0},
        compiler_params=pltpu.CompilerParams(vmem_limit_bytes=48 * 1024 * 1024),
        cost_estimate=pl.CostEstimate(
            flops=2 * tokens * width * TILE * (end - begin),
            bytes_accessed=2 * width * TILE * (end - begin) + 2 * tokens * width,
            transcendentals=0,
        ),
    )(grad, rows_all, *extra)


def add_after(left, right, after):
    def body(*refs):
        total = refs[0][...].astype(F32) + refs[1][...].astype(F32)
        refs[-1][...] = total.astype(BF16)

    return kernel_call(
        body,
        (1,),
        [whole_block(left.shape)] * 2 + [pl.BlockSpec(memory_space=pl.ANY)] * len(after),
        whole_block(left.shape),
        jax.ShapeDtypeStruct(left.shape, BF16),
        left.size,
        8 * left.size,
    )(left, right, *after)


def held_back(value, after):
    def body(*refs):
        refs[-1][...] = refs[0][...]

    return kernel_call(
        body,
        (1,),
        [whole_block(value.shape)] + [pl.BlockSpec(memory_space=pl.ANY)] * len(after),
        whole_block(value.shape),
        jax.ShapeDtypeStruct(value.shape, value.dtype),
        0,
        2 * value.size * value.dtype.itemsize,
    )(value, *after)


def weight_gradient(normed, proj_grad, weight):
    tokens, feat = normed.shape
    cols = proj_grad.shape[1]
    tile = 256 if feat % 256 == 0 else 128

    def body(normed_ref, grad_ref, weight_ref, out_ref, sum_ref):
        grad = contract_first(normed_ref[...], grad_ref[...])
        out_ref[...] = grad.astype(BF16)
        total = jnp.sum(grad * weight_ref[...].astype(F32), axis=1, keepdims=True)
        sum_ref[...] = jnp.broadcast_to(total, sum_ref.shape)

    out, sums = kernel_call(
        body,
        (feat // tile,),
        [
            pl.BlockSpec((tokens, tile), lambda step: (0, step)),
            whole_block((tokens, cols)),
            pl.BlockSpec((tile, cols), lambda step: (step, 0)),
        ],
        [
            pl.BlockSpec((tile, cols), lambda step: (step, 0)),
            pl.BlockSpec((tile, 128), lambda step: (step, 0)),
        ],
        [
            jax.ShapeDtypeStruct((feat, cols), BF16),
            jax.ShapeDtypeStruct((feat, 128), F32),
        ],
        2 * tokens * feat * cols,
        4 * feat * cols + 2 * tokens * (feat + cols),
    )(normed, proj_grad, weight)
    return out, sums[:, 0]


def dot(left, right):
    return jnp.dot(left, right, preferred_element_type=F32)


def cut(array, start, width, axis):
    return lax.dynamic_slice_in_dim(array, start, width, axis)


def local(
    hidden_state,
    embedded_next,
    gain_hidden,
    gain_embed,
    proj_hidden,
    proj_embed,
    final_gain,
    head,
    targets,
    loss_mask,
):
    nc, nv = lax.axis_size("ctx"), lax.axis_size("vocab")
    nx, va = nc // 2, 4
    vb = nv // va
    core = Dim("ctx", nc, 2, 1)
    dim_x = Dim("ctx", nc, nx, 2)
    dim_b = Dim("vocab", nv, vb, 1)
    dim_a = Dim("vocab", nv, va, vb)
    own, slot = lax.axis_index("ctx"), lax.axis_index("vocab")
    x, c, b = own // 2, own % 2, slot % vb

    width = hidden_state.shape[1]
    block = hidden_state.shape[0]
    token_total = targets.shape[0]
    feat, cols = proj_hidden.shape
    half = block // 2
    near = nx * block
    vocab_local = head.shape[0]

    def relative_place(block_index):
        return (c ^ (block_index % 2)) * nx + (x - block_index // 2) % nx

    def block_at(place):
        return ((x - place % nx) % nx) * 2 + (c ^ (place // nx))

    order = jnp.stack([relative_place(jnp.int32(i)) for i in range(nc)])
    to_absolute = (order[:, None] == jnp.arange(nc, dtype=jnp.int32)[None, :])[:, :, None]

    def absolute(value):
        value = value.reshape(value.shape[:-1] + (1, nc, block))
        return jnp.sum(jnp.where(to_absolute, value, 0), axis=-2)

    def relative(value):
        value = jnp.sum(jnp.where(to_absolute, value[..., :, None, :], 0), axis=-3)
        return value.reshape(value.shape[:-2] + (token_total,))

    places = [(rc, rx) for rc in range(2) for rx in range(nx)]

    def send(value, rc, rx):
        pairs = []
        for i in range(nc):
            pairs.append((i, ((i // 2 + rx) % nx) * 2 + ((i % 2) ^ rc)))
        return lax.ppermute(value, "ctx", pairs)

    def scale_of(wide):
        wide = wide.astype(F32)
        return lax.rsqrt(jnp.mean(wide * wide, axis=-1, keepdims=True) + EPSILON)

    def normed_blocks(wide, scale, gain):
        def piece(rc, rx):
            start = (((x + rx) % nx) * 2 + (c ^ rc)) * feat
            value = cut(wide, start, feat, 1).astype(F32)
            return (value * scale * cut(gain, start, feat, 0)).astype(BF16)

        far = {(rc, rx): send(piece(rc, rx), rc, rx) for rx in range(1, nx) for rc in range(2)}
        far[1, 0] = send(piece(1, 0), 1, 0)
        far[0, 0] = piece(0, 0)
        return [far[place] for place in places]

    hidden_scale, embed_scale = scale_of(hidden_state), scale_of(embedded_next)
    blocks_h = normed_blocks(hidden_state, hidden_scale, gain_hidden)
    blocks_e = normed_blocks(embedded_next, embed_scale, gain_embed)

    halves_h = [dot(piece, proj_hidden) for piece in blocks_h]
    halves_e = [dot(piece, proj_embed) for piece in blocks_e]
    projected = halves_h[0] + halves_e[0]
    for index, (rc, rx) in enumerate(places[1:], 1):
        term = (halves_h[index] + halves_e[index]).astype(BF16)
        projected = projected + send(term, rc, (nx - rx) % nx).astype(F32)

    piece = (projected * final_gain).astype(BF16)
    squares = jnp.sum(projected * projected, axis=-1)
    squares = lax.all_to_all(
        jnp.broadcast_to(squares, (nc * nv, block)), ("ctx", "vocab"), 0, 0, tiled=True
    )
    squares = jnp.sum(squares.reshape(nc, nv, block), axis=1)
    row_scale = relative(lax.rsqrt(squares / width + EPSILON))
    pieces = lax.all_gather(piece, ("ctx", "vocab")).reshape(nc, nv, block, cols)
    gathered = jnp.concatenate(
        [
            lax.dynamic_index_in_dim(pieces, block_at(place), 0, keepdims=False)
            .transpose(1, 0, 2)
            .reshape(block, width)
            for place in range(nc)
        ]
    )

    vocab_ids = (own * nv + slot) * vocab_local + lax.iota(jnp.int32, vocab_local)
    logits = contract_last(gathered, head) * row_scale[:, None]
    target = relative(targets.reshape(nc, block))
    mask_weight = loss_mask.astype(F32).reshape(nc, block)
    mask = relative(mask_weight)
    is_target = target[:, None] == vocab_ids[None, :]
    power = jnp.exp(logits)
    sums = jnp.stack(
        [
            jnp.sum(power, axis=-1),
            jnp.sum(power * (logits * F32(1.0 / 256.0)), axis=-1),
            jnp.sum(jnp.where(is_target, logits, F32(0.0)), axis=-1),
        ]
    )
    exp_total, weighted, target_logit = sum_everywhere(absolute(sums))
    log_total = jnp.log(exp_total)
    mean_loss = jnp.sum(mask_weight * (log_total - target_logit)) / token_total
    scaled_dot = mask * relative(weighted / exp_total * F32(256.0) - target_logit)
    probs = jnp.exp(logits - relative(log_total)[:, None])
    scaled_grad = ((mask * row_scale)[:, None] * (probs - is_target.astype(F32))).astype(BF16)
    coefficient = row_scale * row_scale * scaled_dot / width

    def column_chunk(value, place):
        return jnp.stack([cut(value, (p * vb + place) * cols, cols, 1) for p in range(va)])

    theirs = core.swap(dot(scaled_grad[near:], head).astype(BF16), 1)
    mine = lax.optimization_barrier(dot(scaled_grad[:near], head).astype(BF16))
    mine = (mine.astype(F32) + theirs.astype(F32)).astype(BF16)
    mine = mine.reshape(nx, block, width)
    first_sends = [mine[r, :half] for r in range(1, nx)]
    last = mine[:, half:].reshape(nx * half, width)
    last_sends = [column_chunk(last, (b + r) % vb) for r in range(1, vb)]
    first_got = [dim_x.turn(value, -r) for r, value in enumerate(first_sends, 1)]
    last = column_chunk(last, b).astype(F32)
    for r, value in enumerate(last_sends, 1):
        last = last + dim_b.turn(value, r).astype(F32)
    tiles = vocab_local // TILE
    most = max(1, tiles * 3 // 4)
    grad_head, mark = head_gradient(scaled_grad, gathered, (0, most), first_sends + last_sends)
    first = add_after(mine[0, :half], first_got[0], [mark])
    for value in first_got[1:]:
        first = (first.astype(F32) + value.astype(F32)).astype(BF16)
    kept = column_chunk(first, b).astype(F32)
    second_sends = [column_chunk(first, (b + r) % vb) for r in range(1, vb)]
    for r, value in enumerate(second_sends, 1):
        kept = kept + dim_b.turn(value, r).astype(F32)
    first = kept.astype(BF16)
    last = last.astype(BF16).reshape(va, nx, half, cols)
    kept = last[:, 0].astype(F32)
    for r in range(1, nx):
        kept = kept + dim_x.turn(last[:, r], -r).astype(F32)
    grad_head, mark = head_gradient(
        scaled_grad, gathered, (most, tiles), second_sends, base=grad_head
    )
    summed = jnp.concatenate([first, kept.astype(BF16)], axis=1)
    summed = exchange_far(exchange_near(summed, dim_a), dim_a)
    scaled = jnp.concatenate([summed] + [send(summed, rc, rx) for rc, rx in places[1:]])
    scaled = scaled.astype(F32)

    plain = cut(gathered, slot * cols, cols, 1).astype(F32) / final_gain
    grad_final_gain = jnp.sum(scaled * plain, axis=0)
    proj_grad = (scaled * final_gain - plain * coefficient[:, None]).astype(BF16)

    def final_move(value):
        pairs = []
        ratio = nv // nc
        for i in range(nc):
            for j in range(nv):
                pairs.append((i * nv + j, (j // ratio) * nv + i * ratio + j % ratio))
        return lax.ppermute(value, ("ctx", "vocab"), pairs)

    def products(weight, place):
        picked = jnp.concatenate(
            [
                cut(proj_grad, relative_place((p * vb + place) // 2) * block, block, 0)
                for p in range(va)
            ]
        )
        weight_half = cut(weight, (place % 2) * cols, cols, 0)
        return contract_last(picked, weight_half).reshape(va, block, cols)

    def exchanged(weight):
        return [dim_b.swap(products(weight, b ^ r).astype(BF16), r) for r in range(1, vb)]

    got_h, got_e = exchanged(proj_hidden), exchanged(proj_embed)
    kept_h = products(proj_hidden, b)
    for value in got_h:
        kept_h = kept_h + value.astype(F32)
    pair_h = exchange_near(kept_h.astype(BF16), dim_a)
    kept_e = products(proj_embed, b)
    for value in got_e[1:]:
        kept_e = kept_e + value.astype(F32)
    kept_e = add_after(kept_e, got_e[0], [pair_h[1]])
    hidden_moved = final_move(exchange_far(pair_h, dim_a))
    pair_e = exchange_near(kept_e, dim_a)
    hidden_back = hidden_moved.astype(F32)
    embed_back = final_move(exchange_far(pair_e, dim_a)).astype(F32)

    grad_proj_hidden, gain_h = weight_gradient(jnp.concatenate(blocks_h), proj_grad, proj_hidden)
    grad_proj_embed, gain_e = weight_gradient(jnp.concatenate(blocks_e), proj_grad, proj_embed)

    wide = proj_grad.astype(F32).reshape(nc, block, cols)
    dots = jnp.stack(
        [jnp.sum(wide * jnp.stack(halves), axis=-1) for halves in (halves_h, halves_e)]
    )
    dots = jnp.sum(jnp.where(to_absolute, dots[:, None], 0), axis=2)
    dots = jnp.broadcast_to(dots.transpose(1, 0, 2)[:, None], (nc, nv, 2, block))
    gains = jnp.stack([gain_h, gain_e])
    ratio = nv // nc
    gains = gains.reshape(2, ratio, cols).transpose(1, 0, 2)[None]
    holder = jnp.arange(nc, dtype=jnp.int32)[:, None, None, None] == own
    gains = jnp.where(holder, gains, F32(0.0)).reshape(nv, 2, cols)
    gains = jnp.broadcast_to(gains[None], (nc, nv, 2, cols))
    ends = jnp.concatenate([dots, gains], axis=-1).reshape(nc * nv, 2, block + cols)
    ends = held_back(ends, [hidden_moved, pair_e[1]])
    ends = jnp.sum(lax.all_to_all(ends, ("ctx", "vocab"), 0, 0, tiled=True), axis=0)

    def finish(kind, source, gain):
        back_all = (hidden_back, embed_back)[kind]
        scale = (hidden_scale, embed_scale)[kind]
        dot_all = ends[kind, :block][:, None]
        source = cut(source, slot * cols, cols, 1).astype(F32)
        gain = cut(gain, slot * cols, cols, 0)
        grad = scale * (back_all * gain) - source * (scale * scale) * (dot_all / width)
        return grad.astype(BF16), ends[kind, block:] / gain

    grad_hidden, grad_gain_hidden = finish(0, hidden_state, gain_hidden)
    grad_embed, grad_gain_embed = finish(1, embedded_next, gain_embed)
    return (
        mean_loss,
        grad_hidden,
        grad_embed,
        grad_gain_hidden,
        grad_gain_embed,
        grad_proj_hidden,
        grad_proj_embed,
        grad_final_gain,
        grad_head,
    )


def solution(mesh):
    in_specs = (
        P("ctx", None),
        P("ctx", None),
        P(),
        P(),
        P("ctx", "vocab"),
        P("ctx", "vocab"),
        P("vocab"),
        P(("ctx", "vocab"), None),
        P(),
        P(),
    )
    out_specs = (
        P(),
        P("ctx", "vocab"),
        P("ctx", "vocab"),
        P("vocab"),
        P("vocab"),
        P("ctx", "vocab"),
        P("ctx", "vocab"),
        P("vocab"),
        P(("ctx", "vocab"), None),
    )
    return jax.shard_map(local, mesh=mesh, in_specs=in_specs, out_specs=out_specs, check_vma=False)
```

```python
import jax
import jax.numpy as jnp
from jax import lax
from jax.experimental import pallas as pl
from jax.experimental.pallas import tpu as pltpu
from jax.sharding import PartitionSpec as P

EPSILON = 1e-06
TILE = 256
F32 = jnp.float32
BF16 = jnp.bfloat16


class Dim:
    def __init__(self, axis, size, n, stride):
        self.axis, self.size, self.n, self.stride = axis, size, n, stride

    def place(self):
        return (lax.axis_index(self.axis) // self.stride) % self.n

    def move(self, value, target):
        pairs = []
        for index in range(self.size):
            here = (index // self.stride) % self.n
            there = target(here)
            if there is not None and 0 <= there < self.n:
                pairs.append((index, index + (there - here) * self.stride))
        return lax.ppermute(value, self.axis, pairs)

    def swap(self, value, bit):
        return self.move(value, lambda here: here ^ bit)

    def turn(self, value, by):
        return self.move(value, lambda here: (here + by) % self.n)


def exchange_near(chunks, dim):
    here = dim.place()
    pick = [lax.dynamic_index_in_dim(chunks, here ^ bit, 0, keepdims=False) for bit in range(4)]
    got = dim.swap(jnp.stack([pick[1], pick[3]]), 1).astype(F32)
    return pick[0].astype(F32) + got[0], (pick[2].astype(F32) + got[1]).astype(BF16)


def exchange_far(pair, dim):
    near, far = pair
    return (near + dim.swap(far, 2).astype(F32)).astype(BF16)


def sum_everywhere(value):
    axes = ("ctx", "vocab")
    count = lax.axis_size("ctx") * lax.axis_size("vocab")
    copies = jnp.broadcast_to(value[None], (count,) + value.shape)
    return jnp.sum(lax.all_to_all(copies, axes, 0, 0, tiled=True), axis=0)


def contract_first(left, right):
    return lax.dot_general(left, right, (((0,), (0,)), ((), ())), preferred_element_type=F32)


def contract_last(left, right):
    return lax.dot_general(left, right, (((1,), (1,)), ((), ())), preferred_element_type=F32)


def whole_block(shape):
    return pl.BlockSpec(shape, lambda *step: (0,) * len(shape), pipeline_mode=pl.Buffered(1))


def kernel_call(body, grid, in_specs, out_specs, out_shape, flops, moved, exps=0):
    return pl.pallas_call(
        body,
        grid=grid,
        in_specs=in_specs,
        out_specs=out_specs,
        out_shape=out_shape,
        compiler_params=pltpu.CompilerParams(vmem_limit_bytes=48 * 1024 * 1024),
        cost_estimate=pl.CostEstimate(flops=flops, bytes_accessed=moved, transcendentals=exps),
    )


def head_gradient(grad, rows_all, after):
    tokens, entries = grad.shape
    width = rows_all.shape[1]
    chunk = 1024

    def body(grad_ref, rows_ref, *rest):
        out_ref, mark_ref = rest[-2:]
        for start in range(0, width, chunk):
            part = contract_first(grad_ref[...], rows_ref[:, start : start + chunk])
            out_ref[:, start : start + chunk] = part.astype(BF16)
        mark_ref[...] = jnp.zeros_like(mark_ref)

    return pl.pallas_call(
        body,
        grid=(entries // TILE,),
        in_specs=[
            pl.BlockSpec((tokens, TILE), lambda step: (0, step)),
            whole_block((tokens, width)),
        ]
        + [pl.BlockSpec(memory_space=pl.ANY)] * len(after),
        out_specs=[
            pl.BlockSpec((TILE, width), lambda step: (step, 0)),
            pl.BlockSpec((8, 128), lambda step: (0, 0)),
        ],
        out_shape=[
            jax.ShapeDtypeStruct((entries, width), BF16),
            jax.ShapeDtypeStruct((8, 128), F32),
        ],
        compiler_params=pltpu.CompilerParams(vmem_limit_bytes=48 * 1024 * 1024),
        cost_estimate=pl.CostEstimate(
            flops=2 * tokens * width * entries,
            bytes_accessed=2 * width * entries + 2 * tokens * width,
            transcendentals=0,
        ),
    )(grad, rows_all, *after)


def add_after(left, right, after):
    def body(*refs):
        total = refs[0][...].astype(F32) + refs[1][...].astype(F32)
        refs[-1][...] = total.astype(BF16)

    return kernel_call(
        body,
        (1,),
        [whole_block(left.shape)] * 2 + [pl.BlockSpec(memory_space=pl.ANY)] * len(after),
        whole_block(left.shape),
        jax.ShapeDtypeStruct(left.shape, BF16),
        left.size,
        8 * left.size,
    )(left, right, *after)


def held_back(value, after):
    def body(*refs):
        refs[-1][...] = refs[0][...]

    return kernel_call(
        body,
        (1,),
        [whole_block(value.shape)] + [pl.BlockSpec(memory_space=pl.ANY)] * len(after),
        whole_block(value.shape),
        jax.ShapeDtypeStruct(value.shape, value.dtype),
        0,
        2 * value.size * value.dtype.itemsize,
    )(value, *after)


def weight_gradient(normed, proj_grad, weight, after):
    tokens, feat = normed.shape
    cols = proj_grad.shape[1]
    tile = feat // 2 if feat % 256 == 0 and feat // 2 % 128 == 0 else feat

    def body(normed_ref, grad_ref, weight_ref, *rest):
        out_ref, sum_ref = rest[-2:]
        grad = contract_first(normed_ref[...], grad_ref[...])
        out_ref[...] = grad.astype(BF16)
        total = jnp.sum(grad * weight_ref[...].astype(F32), axis=1, keepdims=True)
        sum_ref[...] = jnp.broadcast_to(total, sum_ref.shape)

    out, sums = kernel_call(
        body,
        (feat // tile,),
        [
            pl.BlockSpec((tokens, tile), lambda step: (0, step)),
            whole_block((tokens, cols)),
            pl.BlockSpec((tile, cols), lambda step: (step, 0)),
        ]
        + [pl.BlockSpec(memory_space=pl.ANY)] * len(after),
        [
            pl.BlockSpec((tile, cols), lambda step: (step, 0)),
            pl.BlockSpec((tile, 128), lambda step: (step, 0)),
        ],
        [
            jax.ShapeDtypeStruct((feat, cols), BF16),
            jax.ShapeDtypeStruct((feat, 128), F32),
        ],
        2 * tokens * feat * cols,
        4 * feat * cols + 2 * tokens * (feat + cols),
    )(normed, proj_grad, weight, *after)
    return out, sums[:, 0]


def dot(left, right):
    return jnp.dot(left, right, preferred_element_type=F32)


def cut(array, start, width, axis):
    return lax.dynamic_slice_in_dim(array, start, width, axis)


def local(
    hidden_state,
    embedded_next,
    gain_hidden,
    gain_embed,
    proj_hidden,
    proj_embed,
    final_gain,
    head,
    targets,
    loss_mask,
):
    nc, nv = lax.axis_size("ctx"), lax.axis_size("vocab")
    nx, va = nc // 2, 4
    vb = nv // va
    core = Dim("ctx", nc, 2, 1)
    dim_x = Dim("ctx", nc, nx, 2)
    dim_b = Dim("vocab", nv, vb, 1)
    dim_a = Dim("vocab", nv, va, vb)
    own, slot = lax.axis_index("ctx"), lax.axis_index("vocab")
    x, c, b = own // 2, own % 2, slot % vb

    width = hidden_state.shape[1]
    block = hidden_state.shape[0]
    token_total = targets.shape[0]
    feat, cols = proj_hidden.shape
    half = block // 2
    near = nx * block
    vocab_local = head.shape[0]

    def relative_place(block_index):
        return (c ^ (block_index % 2)) * nx + (x - block_index // 2) % nx

    def block_at(place):
        return ((x - place % nx) % nx) * 2 + (c ^ (place // nx))

    order = jnp.stack([relative_place(jnp.int32(i)) for i in range(nc)])
    to_absolute = (order[:, None] == jnp.arange(nc, dtype=jnp.int32)[None, :])[:, :, None]

    def absolute(value):
        value = value.reshape(value.shape[:-1] + (1, nc, block))
        return jnp.sum(jnp.where(to_absolute, value, 0), axis=-2)

    def relative(value):
        value = jnp.sum(jnp.where(to_absolute, value[..., :, None, :], 0), axis=-3)
        return value.reshape(value.shape[:-2] + (token_total,))

    places = [(rc, rx) for rc in range(2) for rx in range(nx)]

    def send(value, rc, rx):
        pairs = []
        for i in range(nc):
            pairs.append((i, ((i // 2 + rx) % nx) * 2 + ((i % 2) ^ rc)))
        return lax.ppermute(value, "ctx", pairs)

    def scale_of(wide):
        wide = wide.astype(F32)
        return lax.rsqrt(jnp.mean(wide * wide, axis=-1, keepdims=True) + EPSILON)

    def normed_blocks(wide, scale, gain):
        def piece(rc, rx):
            start = (((x + rx) % nx) * 2 + (c ^ rc)) * feat
            value = cut(wide, start, feat, 1).astype(F32)
            return (value * scale * cut(gain, start, feat, 0)).astype(BF16)

        far = {(rc, rx): send(piece(rc, rx), rc, rx) for rx in range(1, nx) for rc in range(2)}
        far[1, 0] = send(piece(1, 0), 1, 0)
        far[0, 0] = piece(0, 0)
        return [far[place] for place in places]

    hidden_scale, embed_scale = scale_of(hidden_state), scale_of(embedded_next)
    blocks_h = normed_blocks(hidden_state, hidden_scale, gain_hidden)
    blocks_e = normed_blocks(embedded_next, embed_scale, gain_embed)

    halves_h = [dot(piece, proj_hidden) for piece in blocks_h]
    halves_e = [dot(piece, proj_embed) for piece in blocks_e]
    projected = halves_h[0] + halves_e[0]
    for index, (rc, rx) in enumerate(places[1:], 1):
        term = (halves_h[index] + halves_e[index]).astype(BF16)
        projected = projected + send(term, rc, (nx - rx) % nx).astype(F32)

    piece = (projected * final_gain).astype(BF16)
    squares = jnp.sum(projected * projected, axis=-1)
    squares = lax.all_to_all(
        jnp.broadcast_to(squares, (nc * nv, block)), ("ctx", "vocab"), 0, 0, tiled=True
    )
    squares = jnp.sum(squares.reshape(nc, nv, block), axis=1)
    row_scale = relative(lax.rsqrt(squares / width + EPSILON))
    pieces = lax.all_gather(piece, ("ctx", "vocab")).reshape(nc, nv, block, cols)
    gathered = jnp.concatenate(
        [
            lax.dynamic_index_in_dim(pieces, block_at(place), 0, keepdims=False)
            .transpose(1, 0, 2)
            .reshape(block, width)
            for place in range(nc)
        ]
    )

    vocab_ids = (own * nv + slot) * vocab_local + lax.iota(jnp.int32, vocab_local)
    logits = contract_last(gathered, head) * row_scale[:, None]
    target = relative(targets.reshape(nc, block))
    mask_weight = loss_mask.astype(F32).reshape(nc, block)
    mask = relative(mask_weight)
    is_target = target[:, None] == vocab_ids[None, :]
    power = jnp.exp(logits)
    sums = jnp.stack(
        [
            jnp.sum(power, axis=-1),
            jnp.sum(power * (logits * F32(1.0 / 256.0)), axis=-1),
            jnp.sum(jnp.where(is_target, logits, F32(0.0)), axis=-1),
        ]
    )
    exp_total, weighted, target_logit = sum_everywhere(absolute(sums))
    log_total = jnp.log(exp_total)
    mean_loss = jnp.sum(mask_weight * (log_total - target_logit)) / token_total
    scaled_dot = mask * relative(weighted / exp_total * F32(256.0) - target_logit)
    probs = jnp.exp(logits - relative(log_total)[:, None])
    scaled_grad = ((mask * row_scale)[:, None] * (probs - is_target.astype(F32))).astype(BF16)
    coefficient = row_scale * row_scale * scaled_dot / width

    def column_chunk(value, place):
        return jnp.stack([cut(value, (p * vb + place) * cols, cols, 1) for p in range(va)])

    theirs = core.swap(dot(scaled_grad[near:], head).astype(BF16), 1)
    mine = lax.optimization_barrier(dot(scaled_grad[:near], head).astype(BF16))
    mine = (mine.astype(F32) + theirs.astype(F32)).astype(BF16)
    mine = mine.reshape(nx, block, width)
    first_sends = [mine[r, :half] for r in range(1, nx)]
    last = mine[:, half:].reshape(nx * half, width)
    last_sends = [column_chunk(last, (b + r) % vb) for r in range(1, vb)]
    first_got = [dim_x.turn(value, -r) for r, value in enumerate(first_sends, 1)]
    last = column_chunk(last, b).astype(F32)
    for r, value in enumerate(last_sends, 1):
        last = last + dim_b.turn(value, r).astype(F32)
    grad_head, mark = head_gradient(scaled_grad, gathered, first_sends + last_sends)
    first = add_after(mine[0, :half], first_got[0], [mark])
    for value in first_got[1:]:
        first = (first.astype(F32) + value.astype(F32)).astype(BF16)
    kept = column_chunk(first, b).astype(F32)
    second_sends = [column_chunk(first, (b + r) % vb) for r in range(1, vb)]
    for r, value in enumerate(second_sends, 1):
        kept = kept + dim_b.turn(value, r).astype(F32)
    first = kept.astype(BF16)
    last = last.astype(BF16).reshape(va, nx, half, cols)
    kept = last[:, 0].astype(F32)
    for r in range(1, nx):
        kept = kept + dim_x.turn(last[:, r], -r).astype(F32)
    summed = jnp.concatenate([first, kept.astype(BF16)], axis=1)
    summed = exchange_far(exchange_near(summed, dim_a), dim_a)
    scaled = jnp.concatenate([summed] + [send(summed, rc, rx) for rc, rx in places[1:]])
    scaled = scaled.astype(F32)

    plain = cut(gathered, slot * cols, cols, 1).astype(F32) / final_gain
    grad_final_gain = jnp.sum(scaled * plain, axis=0)
    proj_grad = (scaled * final_gain - plain * coefficient[:, None]).astype(BF16)

    def final_move(value):
        pairs = []
        ratio = nv // nc
        for i in range(nc):
            for j in range(nv):
                pairs.append((i * nv + j, (j // ratio) * nv + i * ratio + j % ratio))
        return lax.ppermute(value, ("ctx", "vocab"), pairs)

    def products(weight, place):
        picked = jnp.concatenate(
            [
                cut(proj_grad, relative_place((p * vb + place) // 2) * block, block, 0)
                for p in range(va)
            ]
        )
        weight_half = cut(weight, (place % 2) * cols, cols, 0)
        return contract_last(picked, weight_half).reshape(va, block, cols)

    def exchanged(weight):
        return [dim_b.swap(products(weight, b ^ r).astype(BF16), r) for r in range(1, vb)]

    got_h, got_e = exchanged(proj_hidden), exchanged(proj_embed)
    kept_h = products(proj_hidden, b)
    for value in got_h:
        kept_h = kept_h + value.astype(F32)
    kept_h = kept_h.astype(BF16)
    pair_h = exchange_near(kept_h, dim_a)
    kept_e = products(proj_embed, b)
    for value in got_e[1:]:
        kept_e = kept_e + value.astype(F32)
    kept_e = add_after(kept_e, got_e[0], [pair_h[1]])
    hidden_moved = final_move(exchange_far(pair_h, dim_a))
    pair_e = exchange_near(kept_e, dim_a)
    hidden_back = hidden_moved.astype(F32)
    embed_summed = exchange_far(pair_e, dim_a)
    embed_back = final_move(embed_summed).astype(F32)

    grad_proj_hidden, gain_h = weight_gradient(
        jnp.concatenate(blocks_h), proj_grad, proj_hidden, [kept_h]
    )
    grad_proj_embed, gain_e = weight_gradient(
        jnp.concatenate(blocks_e), proj_grad, proj_embed, [pair_h[1]]
    )

    wide = lax.optimization_barrier(proj_grad).astype(F32).reshape(nc, block, cols)
    dots = jnp.stack(
        [jnp.sum(wide * jnp.stack(halves), axis=-1) for halves in (halves_h, halves_e)]
    )
    dots = jnp.sum(jnp.where(to_absolute, dots[:, None], 0), axis=2)
    dots = jnp.broadcast_to(dots.transpose(1, 0, 2)[:, None], (nc, nv, 2, block))
    gains = jnp.stack([gain_h, gain_e])
    ratio = nv // nc
    gains = gains.reshape(2, ratio, cols).transpose(1, 0, 2)[None]
    holder = jnp.arange(nc, dtype=jnp.int32)[:, None, None, None] == own
    gains = jnp.where(holder, gains, F32(0.0)).reshape(nv, 2, cols)
    gains = jnp.broadcast_to(gains[None], (nc, nv, 2, cols))
    ends = jnp.concatenate([dots, gains], axis=-1).reshape(nc * nv, 2, block + cols)
    ends = held_back(ends, [embed_summed, hidden_moved])
    ends = jnp.sum(lax.all_to_all(ends, ("ctx", "vocab"), 0, 0, tiled=True), axis=0)

    def finish(kind, source, gain):
        back_all = (hidden_back, embed_back)[kind]
        scale = (hidden_scale, embed_scale)[kind]
        dot_all = ends[kind, :block][:, None]
        source = cut(source, slot * cols, cols, 1).astype(F32)
        gain = cut(gain, slot * cols, cols, 0)
        grad = scale * (back_all * gain) - source * (scale * scale) * (dot_all / width)
        return grad.astype(BF16), ends[kind, block:] / gain

    grad_hidden, grad_gain_hidden = finish(0, hidden_state, gain_hidden)
    grad_embed, grad_gain_embed = finish(1, embedded_next, gain_embed)
    return (
        mean_loss,
        grad_hidden,
        grad_embed,
        grad_gain_hidden,
        grad_gain_embed,
        grad_proj_hidden,
        grad_proj_embed,
        grad_final_gain,
        grad_head,
    )


def solution(mesh):
    in_specs = (
        P("ctx", None),
        P("ctx", None),
        P(),
        P(),
        P("ctx", "vocab"),
        P("ctx", "vocab"),
        P("vocab"),
        P(("ctx", "vocab"), None),
        P(),
        P(),
    )
    out_specs = (
        P(),
        P("ctx", "vocab"),
        P("ctx", "vocab"),
        P("vocab"),
        P("vocab"),
        P("ctx", "vocab"),
        P("ctx", "vocab"),
        P("vocab"),
        P(("ctx", "vocab"), None),
    )
    return jax.shard_map(local, mesh=mesh, in_specs=in_specs, out_specs=out_specs, check_vma=False)
```

```python
import jax
import jax.numpy as jnp
from jax import lax
from jax.experimental import pallas as pl
from jax.experimental.pallas import tpu as pltpu
from jax.sharding import PartitionSpec as P

EPSILON = 1e-06
TILE = 256
F32 = jnp.float32
BF16 = jnp.bfloat16


class Dim:
    def __init__(self, axis, size, n, stride):
        self.axis, self.size, self.n, self.stride = axis, size, n, stride

    def place(self):
        return (lax.axis_index(self.axis) // self.stride) % self.n

    def move(self, value, target):
        pairs = []
        for index in range(self.size):
            here = (index // self.stride) % self.n
            there = target(here)
            if there is not None and 0 <= there < self.n:
                pairs.append((index, index + (there - here) * self.stride))
        return lax.ppermute(value, self.axis, pairs)

    def swap(self, value, bit):
        return self.move(value, lambda here: here ^ bit)

    def turn(self, value, by):
        return self.move(value, lambda here: (here + by) % self.n)


def exchange_near(chunks, dim):
    here = dim.place()
    pick = [lax.dynamic_index_in_dim(chunks, here ^ bit, 0, keepdims=False) for bit in range(4)]
    sent = jnp.stack([pick[1], pick[3]])
    got = dim.swap(sent, 1).astype(F32)
    return pick[0].astype(F32) + got[0], (pick[2].astype(F32) + got[1]).astype(BF16), sent


def exchange_far(pair, dim):
    near, far = pair[:2]
    return (near + dim.swap(far, 2).astype(F32)).astype(BF16)


def sum_everywhere(value):
    axes = ("ctx", "vocab")
    count = lax.axis_size("ctx") * lax.axis_size("vocab")
    copies = jnp.broadcast_to(value[None], (count,) + value.shape)
    return jnp.sum(lax.all_to_all(copies, axes, 0, 0, tiled=True), axis=0)


def contract_first(left, right):
    return lax.dot_general(left, right, (((0,), (0,)), ((), ())), preferred_element_type=F32)


def contract_last(left, right):
    return lax.dot_general(left, right, (((1,), (1,)), ((), ())), preferred_element_type=F32)


def whole_block(shape):
    return pl.BlockSpec(shape, lambda *step: (0,) * len(shape), pipeline_mode=pl.Buffered(1))


def kernel_call(body, grid, in_specs, out_specs, out_shape, flops, moved, exps=0):
    return pl.pallas_call(
        body,
        grid=grid,
        in_specs=in_specs,
        out_specs=out_specs,
        out_shape=out_shape,
        compiler_params=pltpu.CompilerParams(vmem_limit_bytes=48 * 1024 * 1024),
        cost_estimate=pl.CostEstimate(flops=flops, bytes_accessed=moved, transcendentals=exps),
    )


def head_gradient(grad, rows_all, after):
    tokens, entries = grad.shape
    width = rows_all.shape[1]
    chunk = 1024

    def body(grad_ref, rows_ref, *rest):
        out_ref, mark_ref = rest[-2:]
        for start in range(0, width, chunk):
            part = contract_first(grad_ref[...], rows_ref[:, start : start + chunk])
            out_ref[:, start : start + chunk] = part.astype(BF16)
        mark_ref[...] = jnp.zeros_like(mark_ref)

    return pl.pallas_call(
        body,
        grid=(entries // TILE,),
        in_specs=[
            pl.BlockSpec((tokens, TILE), lambda step: (0, step)),
            whole_block((tokens, width)),
        ]
        + [pl.BlockSpec(memory_space=pl.ANY)] * len(after),
        out_specs=[
            pl.BlockSpec((TILE, width), lambda step: (step, 0)),
            pl.BlockSpec((8, 128), lambda step: (0, 0)),
        ],
        out_shape=[
            jax.ShapeDtypeStruct((entries, width), BF16),
            jax.ShapeDtypeStruct((8, 128), F32),
        ],
        compiler_params=pltpu.CompilerParams(vmem_limit_bytes=48 * 1024 * 1024),
        cost_estimate=pl.CostEstimate(
            flops=2 * tokens * width * entries,
            bytes_accessed=2 * width * entries + 2 * tokens * width,
            transcendentals=0,
        ),
    )(grad, rows_all, *after)


def add_after(left, right, after):
    def body(*refs):
        total = refs[0][...].astype(F32) + refs[1][...].astype(F32)
        refs[-1][...] = total.astype(BF16)

    return kernel_call(
        body,
        (1,),
        [whole_block(left.shape)] * 2 + [pl.BlockSpec(memory_space=pl.ANY)] * len(after),
        whole_block(left.shape),
        jax.ShapeDtypeStruct(left.shape, BF16),
        left.size,
        8 * left.size,
    )(left, right, *after)


def held_back(value, after):
    def body(*refs):
        refs[-1][...] = refs[0][...]

    return kernel_call(
        body,
        (1,),
        [whole_block(value.shape)] + [pl.BlockSpec(memory_space=pl.ANY)] * len(after),
        whole_block(value.shape),
        jax.ShapeDtypeStruct(value.shape, value.dtype),
        0,
        2 * value.size * value.dtype.itemsize,
    )(value, *after)


def weight_gradient(normed, proj_grad, weight, after):
    tokens, feat = normed.shape
    cols = proj_grad.shape[1]
    tile = feat // 2 if feat % 256 == 0 and feat // 2 % 128 == 0 else feat

    def body(normed_ref, grad_ref, weight_ref, *rest):
        out_ref, sum_ref = rest[-2:]
        grad = contract_first(normed_ref[...], grad_ref[...])
        out_ref[...] = grad.astype(BF16)
        total = jnp.sum(grad * weight_ref[...].astype(F32), axis=1, keepdims=True)
        sum_ref[...] = jnp.broadcast_to(total, sum_ref.shape)

    out, sums = kernel_call(
        body,
        (feat // tile,),
        [
            pl.BlockSpec((tokens, tile), lambda step: (0, step)),
            whole_block((tokens, cols)),
            pl.BlockSpec((tile, cols), lambda step: (step, 0)),
        ]
        + [pl.BlockSpec(memory_space=pl.ANY)] * len(after),
        [
            pl.BlockSpec((tile, cols), lambda step: (step, 0)),
            pl.BlockSpec((tile, 128), lambda step: (step, 0)),
        ],
        [
            jax.ShapeDtypeStruct((feat, cols), BF16),
            jax.ShapeDtypeStruct((feat, 128), F32),
        ],
        2 * tokens * feat * cols,
        4 * feat * cols + 2 * tokens * (feat + cols),
    )(normed, proj_grad, weight, *after)
    return out, sums[:, 0]


def dot(left, right):
    return jnp.dot(left, right, preferred_element_type=F32)


def cut(array, start, width, axis):
    return lax.dynamic_slice_in_dim(array, start, width, axis)


def local(
    hidden_state,
    embedded_next,
    gain_hidden,
    gain_embed,
    proj_hidden,
    proj_embed,
    final_gain,
    head,
    targets,
    loss_mask,
):
    nc, nv = lax.axis_size("ctx"), lax.axis_size("vocab")
    nx, va = nc // 2, 4
    vb = nv // va
    core = Dim("ctx", nc, 2, 1)
    dim_x = Dim("ctx", nc, nx, 2)
    dim_b = Dim("vocab", nv, vb, 1)
    dim_a = Dim("vocab", nv, va, vb)
    own, slot = lax.axis_index("ctx"), lax.axis_index("vocab")
    x, c, b = own // 2, own % 2, slot % vb

    width = hidden_state.shape[1]
    block = hidden_state.shape[0]
    token_total = targets.shape[0]
    feat, cols = proj_hidden.shape
    half = block // 2
    near = nx * block
    vocab_local = head.shape[0]

    def relative_place(block_index):
        return (c ^ (block_index % 2)) * nx + (x - block_index // 2) % nx

    def block_at(place):
        return ((x - place % nx) % nx) * 2 + (c ^ (place // nx))

    order = jnp.stack([relative_place(jnp.int32(i)) for i in range(nc)])
    to_absolute = (order[:, None] == jnp.arange(nc, dtype=jnp.int32)[None, :])[:, :, None]

    def absolute(value):
        value = value.reshape(value.shape[:-1] + (1, nc, block))
        return jnp.sum(jnp.where(to_absolute, value, 0), axis=-2)

    def relative(value):
        value = jnp.sum(jnp.where(to_absolute, value[..., :, None, :], 0), axis=-3)
        return value.reshape(value.shape[:-2] + (token_total,))

    places = [(rc, rx) for rc in range(2) for rx in range(nx)]

    def send(value, rc, rx):
        pairs = []
        for i in range(nc):
            pairs.append((i, ((i // 2 + rx) % nx) * 2 + ((i % 2) ^ rc)))
        return lax.ppermute(value, "ctx", pairs)

    def scale_of(wide):
        wide = wide.astype(F32)
        return lax.rsqrt(jnp.mean(wide * wide, axis=-1, keepdims=True) + EPSILON)

    def normed_blocks(wide, scale, gain):
        def piece(rc, rx):
            start = (((x + rx) % nx) * 2 + (c ^ rc)) * feat
            value = cut(wide, start, feat, 1).astype(F32)
            return (value * scale * cut(gain, start, feat, 0)).astype(BF16)

        far = {(rc, rx): send(piece(rc, rx), rc, rx) for rx in range(1, nx) for rc in range(2)}
        far[1, 0] = send(piece(1, 0), 1, 0)
        far[0, 0] = piece(0, 0)
        return [far[place] for place in places]

    hidden_scale, embed_scale = scale_of(hidden_state), scale_of(embedded_next)
    blocks_h = normed_blocks(hidden_state, hidden_scale, gain_hidden)
    blocks_e = normed_blocks(embedded_next, embed_scale, gain_embed)

    halves_h = [dot(piece, proj_hidden) for piece in blocks_h]
    halves_e = [dot(piece, proj_embed) for piece in blocks_e]
    projected = halves_h[0] + halves_e[0]
    for index, (rc, rx) in enumerate(places[1:], 1):
        term = (halves_h[index] + halves_e[index]).astype(BF16)
        projected = projected + send(term, rc, (nx - rx) % nx).astype(F32)

    piece = (projected * final_gain).astype(BF16)
    squares = jnp.sum(projected * projected, axis=-1)
    squares = lax.all_to_all(
        jnp.broadcast_to(squares, (nc * nv, block)), ("ctx", "vocab"), 0, 0, tiled=True
    )
    squares = jnp.sum(squares.reshape(nc, nv, block), axis=1)
    row_scale = relative(lax.rsqrt(squares / width + EPSILON))
    pieces = lax.all_gather(piece, ("ctx", "vocab")).reshape(nc, nv, block, cols)
    gathered = jnp.concatenate(
        [
            lax.dynamic_index_in_dim(pieces, block_at(place), 0, keepdims=False)
            .transpose(1, 0, 2)
            .reshape(block, width)
            for place in range(nc)
        ]
    )

    vocab_ids = (own * nv + slot) * vocab_local + lax.iota(jnp.int32, vocab_local)
    logits = contract_last(gathered, head) * row_scale[:, None]
    target = relative(targets.reshape(nc, block))
    mask_weight = loss_mask.astype(F32).reshape(nc, block)
    mask = relative(mask_weight)
    is_target = target[:, None] == vocab_ids[None, :]
    power = jnp.exp(logits)
    sums = jnp.stack(
        [
            jnp.sum(power, axis=-1),
            jnp.sum(power * (logits * F32(1.0 / 256.0)), axis=-1),
            jnp.sum(jnp.where(is_target, logits, F32(0.0)), axis=-1),
        ]
    )
    exp_total, weighted, target_logit = sum_everywhere(absolute(sums))
    log_total = jnp.log(exp_total)
    mean_loss = jnp.sum(mask_weight * (log_total - target_logit)) / token_total
    scaled_dot = mask * relative(weighted / exp_total * F32(256.0) - target_logit)
    probs = jnp.exp(logits - relative(log_total)[:, None])
    scaled_grad = ((mask * row_scale)[:, None] * (probs - is_target.astype(F32))).astype(BF16)
    coefficient = row_scale * row_scale * scaled_dot / width

    def column_chunk(value, place):
        return jnp.stack([cut(value, (p * vb + place) * cols, cols, 1) for p in range(va)])

    theirs = core.swap(dot(scaled_grad[near:], head).astype(BF16), 1)
    mine = lax.optimization_barrier(dot(scaled_grad[:near], head).astype(BF16))
    mine = (mine.astype(F32) + theirs.astype(F32)).astype(BF16)
    mine = mine.reshape(nx, block, width)
    first_sends = [mine[r, :half] for r in range(1, nx)]
    last = mine[:, half:].reshape(nx * half, width)
    last_sends = [column_chunk(last, (b + r) % vb) for r in range(1, vb)]
    first_got = [dim_x.turn(value, -r) for r, value in enumerate(first_sends, 1)]
    last = column_chunk(last, b).astype(F32)
    for r, value in enumerate(last_sends, 1):
        last = last + dim_b.turn(value, r).astype(F32)
    grad_head, mark = head_gradient(scaled_grad, gathered, first_sends + last_sends)
    first = add_after(mine[0, :half], first_got[0], [mark])
    for value in first_got[1:]:
        first = (first.astype(F32) + value.astype(F32)).astype(BF16)
    kept = column_chunk(first, b).astype(F32)
    second_sends = [column_chunk(first, (b + r) % vb) for r in range(1, vb)]
    for r, value in enumerate(second_sends, 1):
        kept = kept + dim_b.turn(value, r).astype(F32)
    first = kept.astype(BF16)
    last = last.astype(BF16).reshape(va, nx, half, cols)
    kept = last[:, 0].astype(F32)
    for r in range(1, nx):
        kept = kept + dim_x.turn(last[:, r], -r).astype(F32)
    summed = jnp.concatenate([first, kept.astype(BF16)], axis=1)
    summed = exchange_far(exchange_near(summed, dim_a), dim_a)
    scaled = jnp.concatenate([summed] + [send(summed, rc, rx) for rc, rx in places[1:]])
    scaled = scaled.astype(F32)

    plain = cut(gathered, slot * cols, cols, 1).astype(F32) / final_gain
    grad_final_gain = jnp.sum(scaled * plain, axis=0)
    proj_grad = (scaled * final_gain - plain * coefficient[:, None]).astype(BF16)

    def final_move(value):
        pairs = []
        ratio = nv // nc
        for i in range(nc):
            for j in range(nv):
                pairs.append((i * nv + j, (j // ratio) * nv + i * ratio + j % ratio))
        return lax.ppermute(value, ("ctx", "vocab"), pairs)

    def products(weight, place):
        picked = jnp.concatenate(
            [
                cut(proj_grad, relative_place((p * vb + place) // 2) * block, block, 0)
                for p in range(va)
            ]
        )
        weight_half = cut(weight, (place % 2) * cols, cols, 0)
        return contract_last(picked, weight_half).reshape(va, block, cols)

    if vb == nv // nc:
        def half_weight(weight, place):
            return cut(weight, place * cols, cols, 0)

        def along_b(weight):
            return [
                dim_b.swap(contract_last(proj_grad, half_weight(weight, b ^ r)).astype(BF16), r)
                for r in range(1, vb)
            ]

        def to_owners(value):
            value = value.reshape(nc, block, cols)
            moved = [
                send(value[index], rc, (nx - rx) % nx)
                for index, (rc, rx) in enumerate(places[1:], 1)
            ]
            return [value[0]] + moved

        def by_holder(pieces):
            at = [(c ^ (i % 2)) * nx + (i // 2 - x) % nx for i in range(nc)]
            stack = jnp.stack(pieces)
            return jnp.stack(
                [lax.dynamic_index_in_dim(stack, at[i], 0, keepdims=False) for i in range(nc)]
            )

        got_h, got_e = along_b(proj_hidden), along_b(proj_embed)
        kept_h = contract_last(proj_grad, half_weight(proj_hidden, b))
        for value in got_h:
            kept_h = kept_h + value.astype(F32)
        kept_h = kept_h.astype(BF16)
        owned_h = to_owners(kept_h)
        pair_h = exchange_near(by_holder(owned_h), dim_a)
        kept_e = contract_last(proj_grad, half_weight(proj_embed, b))
        for value in got_e[1:]:
            kept_e = kept_e + value.astype(F32)
        kept_e = add_after(kept_e, got_e[0], [pair_h[2]])
        owned_e = to_owners(kept_e)
        marks = [kept_h], [pair_h[2]], [owned_e[nx], pair_h[1]]
        owned_e[nx] = held_back(owned_e[nx], [pair_h[1]])
        hidden_back = exchange_far(pair_h, dim_a).astype(F32)
        embed_back = exchange_far(exchange_near(by_holder(owned_e), dim_a), dim_a).astype(F32)
    else:
        got_h, got_e = [
            [dim_b.swap(products(weight, b ^ r).astype(BF16), r) for r in range(1, vb)]
            for weight in (proj_hidden, proj_embed)
        ]
        kept_h, kept_e = products(proj_hidden, b), products(proj_embed, b)
        for value_h, value_e in zip(got_h, got_e):
            kept_h = kept_h + value_h.astype(F32)
            kept_e = kept_e + value_e.astype(F32)
        pair_h = exchange_near(kept_h.astype(BF16), dim_a)
        pair_e = exchange_near(kept_e.astype(BF16), dim_a)
        hidden_back = final_move(exchange_far(pair_h, dim_a)).astype(F32)
        embed_back = final_move(exchange_far(pair_e, dim_a)).astype(F32)
        marks = [proj_grad], [proj_grad], [proj_grad]

    grad_proj_hidden, gain_h = weight_gradient(
        jnp.concatenate(blocks_h), proj_grad, proj_hidden, marks[0]
    )
    grad_proj_embed, gain_e = weight_gradient(
        jnp.concatenate(blocks_e), proj_grad, proj_embed, marks[1]
    )

    wide = lax.optimization_barrier(proj_grad).astype(F32).reshape(nc, block, cols)
    dots = jnp.stack(
        [jnp.sum(wide * jnp.stack(halves), axis=-1) for halves in (halves_h, halves_e)]
    )
    dots = jnp.sum(jnp.where(to_absolute, dots[:, None], 0), axis=2)
    dots = jnp.broadcast_to(dots.transpose(1, 0, 2)[:, None], (nc, nv, 2, block))
    gains = jnp.stack([gain_h, gain_e])
    ratio = nv // nc
    gains = gains.reshape(2, ratio, cols).transpose(1, 0, 2)[None]
    holder = jnp.arange(nc, dtype=jnp.int32)[:, None, None, None] == own
    gains = jnp.where(holder, gains, F32(0.0)).reshape(nv, 2, cols)
    gains = jnp.broadcast_to(gains[None], (nc, nv, 2, cols))
    ends = jnp.concatenate([dots, gains], axis=-1).reshape(nc * nv, 2, block + cols)
    ends = held_back(ends, marks[2])
    ends = jnp.sum(lax.all_to_all(ends, ("ctx", "vocab"), 0, 0, tiled=True), axis=0)

    def finish(kind, source, gain):
        back_all = (hidden_back, embed_back)[kind]
        scale = (hidden_scale, embed_scale)[kind]
        dot_all = ends[kind, :block][:, None]
        source = cut(source, slot * cols, cols, 1).astype(F32)
        gain = cut(gain, slot * cols, cols, 0)
        grad = scale * (back_all * gain) - source * (scale * scale) * (dot_all / width)
        return grad.astype(BF16), ends[kind, block:] / gain

    grad_hidden, grad_gain_hidden = finish(0, hidden_state, gain_hidden)
    grad_embed, grad_gain_embed = finish(1, embedded_next, gain_embed)
    return (
        mean_loss,
        grad_hidden,
        grad_embed,
        grad_gain_hidden,
        grad_gain_embed,
        grad_proj_hidden,
        grad_proj_embed,
        grad_final_gain,
        grad_head,
    )


def solution(mesh):
    in_specs = (
        P("ctx", None),
        P("ctx", None),
        P(),
        P(),
        P("ctx", "vocab"),
        P("ctx", "vocab"),
        P("vocab"),
        P(("ctx", "vocab"), None),
        P(),
        P(),
    )
    out_specs = (
        P(),
        P("ctx", "vocab"),
        P("ctx", "vocab"),
        P("vocab"),
        P("vocab"),
        P("ctx", "vocab"),
        P("ctx", "vocab"),
        P("vocab"),
        P(("ctx", "vocab"), None),
    )
    return jax.shard_map(local, mesh=mesh, in_specs=in_specs, out_specs=out_specs, check_vma=False)
```

```python
import jax
import jax.numpy as jnp
from jax import lax
from jax.experimental import pallas as pl
from jax.experimental.pallas import tpu as pltpu
from jax.sharding import PartitionSpec as P

EPSILON = 1e-06
TILE = 256
F32 = jnp.float32
BF16 = jnp.bfloat16


class Dim:
    def __init__(self, axis, size, n, stride):
        self.axis, self.size, self.n, self.stride = axis, size, n, stride

    def place(self):
        return (lax.axis_index(self.axis) // self.stride) % self.n

    def move(self, value, target):
        pairs = []
        for index in range(self.size):
            here = (index // self.stride) % self.n
            there = target(here)
            if there is not None and 0 <= there < self.n:
                pairs.append((index, index + (there - here) * self.stride))
        return lax.ppermute(value, self.axis, pairs)

    def swap(self, value, bit):
        return self.move(value, lambda here: here ^ bit)

    def turn(self, value, by):
        return self.move(value, lambda here: (here + by) % self.n)


def exchange_near(chunks, dim):
    here = dim.place()
    pick = [lax.dynamic_index_in_dim(chunks, here ^ bit, 0, keepdims=False) for bit in range(4)]
    sent = jnp.stack([pick[1], pick[3]])
    got = dim.swap(sent, 1).astype(F32)
    return pick[0].astype(F32) + got[0], (pick[2].astype(F32) + got[1]).astype(BF16), sent


def exchange_far(pair, dim):
    near, far = pair[:2]
    return (near + dim.swap(far, 2).astype(F32)).astype(BF16)


def sum_everywhere(value):
    axes = ("ctx", "vocab")
    count = lax.axis_size("ctx") * lax.axis_size("vocab")
    copies = jnp.broadcast_to(value[None], (count,) + value.shape)
    return jnp.sum(lax.all_to_all(copies, axes, 0, 0, tiled=True), axis=0)


def contract_first(left, right):
    return lax.dot_general(left, right, (((0,), (0,)), ((), ())), preferred_element_type=F32)


def contract_last(left, right):
    return lax.dot_general(left, right, (((1,), (1,)), ((), ())), preferred_element_type=F32)


def whole_block(shape):
    return pl.BlockSpec(shape, lambda *step: (0,) * len(shape), pipeline_mode=pl.Buffered(1))


def kernel_call(body, grid, in_specs, out_specs, out_shape, flops, moved, exps=0):
    return pl.pallas_call(
        body,
        grid=grid,
        in_specs=in_specs,
        out_specs=out_specs,
        out_shape=out_shape,
        compiler_params=pltpu.CompilerParams(vmem_limit_bytes=48 * 1024 * 1024),
        cost_estimate=pl.CostEstimate(flops=flops, bytes_accessed=moved, transcendentals=exps),
    )


def head_gradient(grad, rows_all, after):
    tokens, entries = grad.shape
    width = rows_all.shape[1]
    chunk = 1024

    def body(grad_ref, rows_ref, *rest):
        out_ref, mark_ref = rest[-2:]
        for start in range(0, width, chunk):
            part = contract_first(grad_ref[...], rows_ref[:, start : start + chunk])
            out_ref[:, start : start + chunk] = part.astype(BF16)
        mark_ref[...] = jnp.zeros_like(mark_ref)

    return pl.pallas_call(
        body,
        grid=(entries // TILE,),
        in_specs=[
            pl.BlockSpec((tokens, TILE), lambda step: (0, step)),
            whole_block((tokens, width)),
        ]
        + [pl.BlockSpec(memory_space=pl.ANY)] * len(after),
        out_specs=[
            pl.BlockSpec((TILE, width), lambda step: (step, 0)),
            pl.BlockSpec((8, 128), lambda step: (0, 0)),
        ],
        out_shape=[
            jax.ShapeDtypeStruct((entries, width), BF16),
            jax.ShapeDtypeStruct((8, 128), F32),
        ],
        compiler_params=pltpu.CompilerParams(vmem_limit_bytes=48 * 1024 * 1024),
        cost_estimate=pl.CostEstimate(
            flops=2 * tokens * width * entries,
            bytes_accessed=2 * width * entries + 2 * tokens * width,
            transcendentals=0,
        ),
    )(grad, rows_all, *after)


def add_after(left, right, after):
    def body(*refs):
        total = refs[0][...].astype(F32) + refs[1][...].astype(F32)
        refs[-1][...] = total.astype(BF16)

    return kernel_call(
        body,
        (1,),
        [whole_block(left.shape)] * 2 + [pl.BlockSpec(memory_space=pl.ANY)] * len(after),
        whole_block(left.shape),
        jax.ShapeDtypeStruct(left.shape, BF16),
        left.size,
        8 * left.size,
    )(left, right, *after)


def held_back(value, after):
    def body(*refs):
        refs[-1][...] = refs[0][...]

    return kernel_call(
        body,
        (1,),
        [whole_block(value.shape)] + [pl.BlockSpec(memory_space=pl.ANY)] * len(after),
        whole_block(value.shape),
        jax.ShapeDtypeStruct(value.shape, value.dtype),
        0,
        2 * value.size * value.dtype.itemsize,
    )(value, *after)


def weight_gradient(normed, proj_grad, weight, after):
    tokens, feat = normed.shape
    cols = proj_grad.shape[1]
    tile = feat // 2 if feat % 256 == 0 and feat // 2 % 128 == 0 else feat

    def body(normed_ref, grad_ref, weight_ref, *rest):
        out_ref, sum_ref = rest[-2:]
        grad = contract_first(normed_ref[...], grad_ref[...])
        out_ref[...] = grad.astype(BF16)
        total = jnp.sum(grad * weight_ref[...].astype(F32), axis=1, keepdims=True)
        sum_ref[...] = jnp.broadcast_to(total, sum_ref.shape)

    out, sums = kernel_call(
        body,
        (feat // tile,),
        [
            pl.BlockSpec((tokens, tile), lambda step: (0, step)),
            whole_block((tokens, cols)),
            pl.BlockSpec((tile, cols), lambda step: (step, 0)),
        ]
        + [pl.BlockSpec(memory_space=pl.ANY)] * len(after),
        [
            pl.BlockSpec((tile, cols), lambda step: (step, 0)),
            pl.BlockSpec((tile, 128), lambda step: (step, 0)),
        ],
        [
            jax.ShapeDtypeStruct((feat, cols), BF16),
            jax.ShapeDtypeStruct((feat, 128), F32),
        ],
        2 * tokens * feat * cols,
        4 * feat * cols + 2 * tokens * (feat + cols),
    )(normed, proj_grad, weight, *after)
    return out, sums[:, 0]


def dot(left, right):
    return jnp.dot(left, right, preferred_element_type=F32)


def cut(array, start, width, axis):
    return lax.dynamic_slice_in_dim(array, start, width, axis)


def local(
    hidden_state,
    embedded_next,
    gain_hidden,
    gain_embed,
    proj_hidden,
    proj_embed,
    final_gain,
    head,
    targets,
    loss_mask,
):
    nc, nv = lax.axis_size("ctx"), lax.axis_size("vocab")
    nx, va = nc // 2, 4
    vb = nv // va
    core = Dim("ctx", nc, 2, 1)
    dim_x = Dim("ctx", nc, nx, 2)
    dim_b = Dim("vocab", nv, vb, 1)
    dim_a = Dim("vocab", nv, va, vb)
    own, slot = lax.axis_index("ctx"), lax.axis_index("vocab")
    x, c, b = own // 2, own % 2, slot % vb

    width = hidden_state.shape[1]
    block = hidden_state.shape[0]
    token_total = targets.shape[0]
    feat, cols = proj_hidden.shape
    half = block // 2
    near = nx * block
    vocab_local = head.shape[0]

    def relative_place(block_index):
        return (c ^ (block_index % 2)) * nx + (x - block_index // 2) % nx

    def block_at(place):
        return ((x - place % nx) % nx) * 2 + (c ^ (place // nx))

    order = jnp.stack([relative_place(jnp.int32(i)) for i in range(nc)])
    to_absolute = (order[:, None] == jnp.arange(nc, dtype=jnp.int32)[None, :])[:, :, None]

    def absolute(value):
        value = value.reshape(value.shape[:-1] + (1, nc, block))
        return jnp.sum(jnp.where(to_absolute, value, 0), axis=-2)

    def relative(value):
        value = jnp.sum(jnp.where(to_absolute, value[..., :, None, :], 0), axis=-3)
        return value.reshape(value.shape[:-2] + (token_total,))

    places = [(rc, rx) for rc in range(2) for rx in range(nx)]

    def send(value, rc, rx):
        pairs = []
        for i in range(nc):
            pairs.append((i, ((i // 2 + rx) % nx) * 2 + ((i % 2) ^ rc)))
        return lax.ppermute(value, "ctx", pairs)

    def scale_of(wide):
        wide = wide.astype(F32)
        return lax.rsqrt(jnp.mean(wide * wide, axis=-1, keepdims=True) + EPSILON)

    def normed_piece(wide, scale, gain, rc, rx):
        start = (((x + rx) % nx) * 2 + (c ^ rc)) * feat
        value = cut(wide, start, feat, 1).astype(F32)
        return (value * scale * cut(gain, start, feat, 0)).astype(BF16)

    hidden_scale, embed_scale = scale_of(hidden_state), scale_of(embedded_next)
    even = b % 2 == 0
    far_h, far_e = {}, {}
    for rx in range(nx):
        for rc in range(2):
            piece_h = normed_piece(hidden_state, hidden_scale, gain_hidden, rc, rx)
            piece_e = normed_piece(embedded_next, embed_scale, gain_embed, rc, rx)
            if rx == 0:
                far_h[rc, 0] = send(piece_h, rc, 0) if rc else piece_h
                far_e[rc, 0] = send(piece_e, rc, 0) if rc else piece_e
                continue
            got = send(jnp.where(even, piece_h, piece_e), rc, rx)
            twin = dim_b.swap(got, 1)
            far_h[rc, rx] = jnp.where(even, got, twin)
            far_e[rc, rx] = jnp.where(even, twin, got)
    blocks_h = [far_h[place] for place in places]
    blocks_e = [far_e[place] for place in places]

    halves_h = [dot(piece, proj_hidden) for piece in blocks_h]
    halves_e = [dot(piece, proj_embed) for piece in blocks_e]
    projected = halves_h[0] + halves_e[0]
    for index, (rc, rx) in enumerate(places[1:], 1):
        term = (halves_h[index] + halves_e[index]).astype(BF16)
        projected = projected + send(term, rc, (nx - rx) % nx).astype(F32)

    piece = (projected * final_gain).astype(BF16)
    squares = jnp.sum(projected * projected, axis=-1)
    squares = lax.all_to_all(
        jnp.broadcast_to(squares, (nc * nv, block)), ("ctx", "vocab"), 0, 0, tiled=True
    )
    squares = jnp.sum(squares.reshape(nc, nv, block), axis=1)
    row_scale = relative(lax.rsqrt(squares / width + EPSILON))
    pieces = lax.all_gather(piece, ("ctx", "vocab")).reshape(nc, nv, block, cols)
    gathered = jnp.concatenate(
        [
            lax.dynamic_index_in_dim(pieces, block_at(place), 0, keepdims=False)
            .transpose(1, 0, 2)
            .reshape(block, width)
            for place in range(nc)
        ]
    )

    vocab_ids = (own * nv + slot) * vocab_local + lax.iota(jnp.int32, vocab_local)
    logits = contract_last(gathered, head) * row_scale[:, None]
    target = relative(targets.reshape(nc, block))
    mask_weight = loss_mask.astype(F32).reshape(nc, block)
    mask = relative(mask_weight)
    is_target = target[:, None] == vocab_ids[None, :]
    power = jnp.exp(logits)
    sums = jnp.stack(
        [
            jnp.sum(power, axis=-1),
            jnp.sum(power * (logits * F32(1.0 / 256.0)), axis=-1),
            jnp.sum(jnp.where(is_target, logits, F32(0.0)), axis=-1),
        ]
    )
    exp_total, weighted, target_logit = sum_everywhere(absolute(sums))
    log_total = jnp.log(exp_total)
    mean_loss = jnp.sum(mask_weight * (log_total - target_logit)) / token_total
    scaled_dot = mask * relative(weighted / exp_total * F32(256.0) - target_logit)
    probs = jnp.exp(logits - relative(log_total)[:, None])
    scaled_grad = ((mask * row_scale)[:, None] * (probs - is_target.astype(F32))).astype(BF16)
    coefficient = row_scale * row_scale * scaled_dot / width

    def column_chunk(value, place):
        return jnp.stack([cut(value, (p * vb + place) * cols, cols, 1) for p in range(va)])

    theirs = core.swap(dot(scaled_grad[near:], head).astype(BF16), 1)
    mine = lax.optimization_barrier(dot(scaled_grad[:near], head).astype(BF16))
    mine = (mine.astype(F32) + theirs.astype(F32)).astype(BF16)
    mine = mine.reshape(nx, block, width)
    first_sends = [mine[r, :half] for r in range(1, nx)]
    last = mine[:, half:].reshape(nx * half, width)
    last_sends = [column_chunk(last, (b + r) % vb) for r in range(1, vb)]
    first_got = [dim_x.turn(value, -r) for r, value in enumerate(first_sends, 1)]
    last = column_chunk(last, b).astype(F32)
    for r, value in enumerate(last_sends, 1):
        last = last + dim_b.turn(value, r).astype(F32)
    grad_head, mark = head_gradient(scaled_grad, gathered, first_sends + last_sends)
    first = add_after(mine[0, :half], first_got[0], [mark])
    for value in first_got[1:]:
        first = (first.astype(F32) + value.astype(F32)).astype(BF16)
    kept = column_chunk(first, b).astype(F32)
    second_sends = [column_chunk(first, (b + r) % vb) for r in range(1, vb)]
    for r, value in enumerate(second_sends, 1):
        kept = kept + dim_b.turn(value, r).astype(F32)
    first = kept.astype(BF16)
    last = last.astype(BF16).reshape(va, nx, half, cols)
    kept = last[:, 0].astype(F32)
    for r in range(1, nx):
        kept = kept + dim_x.turn(last[:, r], -r).astype(F32)
    summed = jnp.concatenate([first, kept.astype(BF16)], axis=1)
    summed = exchange_far(exchange_near(summed, dim_a), dim_a)
    scaled = jnp.concatenate([summed] + [send(summed, rc, rx) for rc, rx in places[1:]])
    scaled = scaled.astype(F32)

    plain = cut(gathered, slot * cols, cols, 1).astype(F32) / final_gain
    grad_final_gain = jnp.sum(scaled * plain, axis=0)
    proj_grad = (scaled * final_gain - plain * coefficient[:, None]).astype(BF16)

    def final_move(value):
        pairs = []
        ratio = nv // nc
        for i in range(nc):
            for j in range(nv):
                pairs.append((i * nv + j, (j // ratio) * nv + i * ratio + j % ratio))
        return lax.ppermute(value, ("ctx", "vocab"), pairs)

    def products(weight, place):
        picked = jnp.concatenate(
            [
                cut(proj_grad, relative_place((p * vb + place) // 2) * block, block, 0)
                for p in range(va)
            ]
        )
        weight_half = cut(weight, (place % 2) * cols, cols, 0)
        return contract_last(picked, weight_half).reshape(va, block, cols)

    if vb == nv // nc:
        def half_weight(weight, place):
            return cut(weight, place * cols, cols, 0)

        def along_b(weight):
            return [
                dim_b.swap(contract_last(proj_grad, half_weight(weight, b ^ r)).astype(BF16), r)
                for r in range(1, vb)
            ]

        def to_owners(value):
            value = value.reshape(nc, block, cols)
            moved = [
                send(value[index], rc, (nx - rx) % nx)
                for index, (rc, rx) in enumerate(places[1:], 1)
            ]
            return [value[0]] + moved

        def by_holder(pieces):
            at = [(c ^ (i % 2)) * nx + (i // 2 - x) % nx for i in range(nc)]
            stack = jnp.stack(pieces)
            return jnp.stack(
                [lax.dynamic_index_in_dim(stack, at[i], 0, keepdims=False) for i in range(nc)]
            )

        got_h, got_e = along_b(proj_hidden), along_b(proj_embed)
        kept_h = contract_last(proj_grad, half_weight(proj_hidden, b))
        for value in got_h:
            kept_h = kept_h + value.astype(F32)
        kept_h = kept_h.astype(BF16)
        owned_h = to_owners(kept_h)
        pair_h = exchange_near(by_holder(owned_h), dim_a)
        kept_e = contract_last(proj_grad, half_weight(proj_embed, b))
        for value in got_e[1:]:
            kept_e = kept_e + value.astype(F32)
        kept_e = add_after(kept_e, got_e[0], [pair_h[2]])
        owned_e = to_owners(kept_e)
        owned_e[nx] = held_back(owned_e[nx], [pair_h[1]])
        hidden_summed = exchange_far(pair_h, dim_a)
        hidden_back = hidden_summed.astype(F32)
        marks = [kept_h], [pair_h[2]], [owned_e[nx], hidden_summed]
        embed_back = exchange_far(exchange_near(by_holder(owned_e), dim_a), dim_a).astype(F32)
    else:
        got_h, got_e = [
            [dim_b.swap(products(weight, b ^ r).astype(BF16), r) for r in range(1, vb)]
            for weight in (proj_hidden, proj_embed)
        ]
        kept_h, kept_e = products(proj_hidden, b), products(proj_embed, b)
        for value_h, value_e in zip(got_h, got_e):
            kept_h = kept_h + value_h.astype(F32)
            kept_e = kept_e + value_e.astype(F32)
        pair_h = exchange_near(kept_h.astype(BF16), dim_a)
        pair_e = exchange_near(kept_e.astype(BF16), dim_a)
        hidden_back = final_move(exchange_far(pair_h, dim_a)).astype(F32)
        embed_back = final_move(exchange_far(pair_e, dim_a)).astype(F32)
        marks = [proj_grad], [proj_grad], [proj_grad]

    grad_proj_hidden, gain_h = weight_gradient(
        jnp.concatenate(blocks_h), proj_grad, proj_hidden, marks[0]
    )
    grad_proj_embed, gain_e = weight_gradient(
        jnp.concatenate(blocks_e), proj_grad, proj_embed, marks[1]
    )

    wide = lax.optimization_barrier(proj_grad).astype(F32).reshape(nc, block, cols)
    dots = jnp.stack(
        [jnp.sum(wide * jnp.stack(halves), axis=-1) for halves in (halves_h, halves_e)]
    )
    dots = jnp.sum(jnp.where(to_absolute, dots[:, None], 0), axis=2)
    dots = jnp.broadcast_to(dots.transpose(1, 0, 2)[:, None], (nc, nv, 2, block))
    gains = jnp.stack([gain_h, gain_e])
    ratio = nv // nc
    gains = gains.reshape(2, ratio, cols).transpose(1, 0, 2)[None]
    holder = jnp.arange(nc, dtype=jnp.int32)[:, None, None, None] == own
    gains = jnp.where(holder, gains, F32(0.0)).reshape(nv, 2, cols)
    gains = jnp.broadcast_to(gains[None], (nc, nv, 2, cols))
    ends = jnp.concatenate([dots, gains], axis=-1).reshape(nc * nv, 2, block + cols)
    ends = held_back(ends, marks[2])
    ends = jnp.sum(lax.all_to_all(ends, ("ctx", "vocab"), 0, 0, tiled=True), axis=0)

    def finish(kind, source, gain):
        back_all = (hidden_back, embed_back)[kind]
        scale = (hidden_scale, embed_scale)[kind]
        dot_all = ends[kind, :block][:, None]
        source = cut(source, slot * cols, cols, 1).astype(F32)
        gain = cut(gain, slot * cols, cols, 0)
        grad = scale * (back_all * gain) - source * (scale * scale) * (dot_all / width)
        return grad.astype(BF16), ends[kind, block:] / gain

    grad_hidden, grad_gain_hidden = finish(0, hidden_state, gain_hidden)
    grad_embed, grad_gain_embed = finish(1, embedded_next, gain_embed)
    return (
        mean_loss,
        grad_hidden,
        grad_embed,
        grad_gain_hidden,
        grad_gain_embed,
        grad_proj_hidden,
        grad_proj_embed,
        grad_final_gain,
        grad_head,
    )


def solution(mesh):
    in_specs = (
        P("ctx", None),
        P("ctx", None),
        P(),
        P(),
        P("ctx", "vocab"),
        P("ctx", "vocab"),
        P("vocab"),
        P(("ctx", "vocab"), None),
        P(),
        P(),
    )
    out_specs = (
        P(),
        P("ctx", "vocab"),
        P("ctx", "vocab"),
        P("vocab"),
        P("vocab"),
        P("ctx", "vocab"),
        P("ctx", "vocab"),
        P("vocab"),
        P(("ctx", "vocab"), None),
    )
    return jax.shard_map(local, mesh=mesh, in_specs=in_specs, out_specs=out_specs, check_vma=False)
```

```python
import jax
import jax.numpy as jnp
from jax import lax
from jax.experimental import pallas as pl
from jax.experimental.pallas import tpu as pltpu
from jax.sharding import PartitionSpec as P

EPSILON = 1e-06
TILE = 256
F32 = jnp.float32
BF16 = jnp.bfloat16


class Dim:
    def __init__(self, axis, size, n, stride):
        self.axis, self.size, self.n, self.stride = axis, size, n, stride

    def place(self):
        return (lax.axis_index(self.axis) // self.stride) % self.n

    def move(self, value, target):
        pairs = []
        for index in range(self.size):
            here = (index // self.stride) % self.n
            there = target(here)
            if there is not None and 0 <= there < self.n:
                pairs.append((index, index + (there - here) * self.stride))
        return lax.ppermute(value, self.axis, pairs)

    def swap(self, value, bit):
        return self.move(value, lambda here: here ^ bit)

    def turn(self, value, by):
        return self.move(value, lambda here: (here + by) % self.n)


def exchange_near(chunks, dim):
    here = dim.place()
    pick = [lax.dynamic_index_in_dim(chunks, here ^ bit, 0, keepdims=False) for bit in range(4)]
    sent = jnp.stack([pick[1], pick[3]])
    got = dim.swap(sent, 1).astype(F32)
    return pick[0].astype(F32) + got[0], (pick[2].astype(F32) + got[1]).astype(BF16), sent


def exchange_far(pair, dim):
    near, far = pair[:2]
    return (near + dim.swap(far, 2).astype(F32)).astype(BF16)


def sum_everywhere(value):
    axes = ("ctx", "vocab")
    count = lax.axis_size("ctx") * lax.axis_size("vocab")
    copies = jnp.broadcast_to(value[None], (count,) + value.shape)
    return jnp.sum(lax.all_to_all(copies, axes, 0, 0, tiled=True), axis=0)


def contract_first(left, right):
    return lax.dot_general(left, right, (((0,), (0,)), ((), ())), preferred_element_type=F32)


def contract_last(left, right):
    return lax.dot_general(left, right, (((1,), (1,)), ((), ())), preferred_element_type=F32)


def whole_block(shape):
    return pl.BlockSpec(shape, lambda *step: (0,) * len(shape), pipeline_mode=pl.Buffered(1))


def kernel_call(body, grid, in_specs, out_specs, out_shape, flops, moved, exps=0):
    return pl.pallas_call(
        body,
        grid=grid,
        in_specs=in_specs,
        out_specs=out_specs,
        out_shape=out_shape,
        compiler_params=pltpu.CompilerParams(vmem_limit_bytes=48 * 1024 * 1024),
        cost_estimate=pl.CostEstimate(flops=flops, bytes_accessed=moved, transcendentals=exps),
    )


def head_gradient(grads, rows_all, after):
    tokens, entries = grads[0].shape
    width = rows_all[0].shape[1]
    chunk = 1024

    def body(near_ref, far_ref, near_rows_ref, far_rows_ref, *rest):
        out_ref, mark_ref = rest[-2:]
        for start in range(0, width, chunk):
            part = contract_first(near_ref[...], near_rows_ref[:, start : start + chunk])
            part += contract_first(far_ref[...], far_rows_ref[:, start : start + chunk])
            out_ref[:, start : start + chunk] = part.astype(BF16)
        mark_ref[...] = jnp.zeros_like(mark_ref)

    return pl.pallas_call(
        body,
        grid=(entries // TILE,),
        in_specs=[
            pl.BlockSpec((tokens, TILE), lambda step: (0, step)),
            pl.BlockSpec((tokens, TILE), lambda step: (0, step)),
            whole_block((tokens, width)),
            whole_block((tokens, width)),
        ]
        + [pl.BlockSpec(memory_space=pl.ANY)] * len(after),
        out_specs=[
            pl.BlockSpec((TILE, width), lambda step: (step, 0)),
            pl.BlockSpec((8, 128), lambda step: (0, 0)),
        ],
        out_shape=[
            jax.ShapeDtypeStruct((entries, width), BF16),
            jax.ShapeDtypeStruct((8, 128), F32),
        ],
        compiler_params=pltpu.CompilerParams(vmem_limit_bytes=48 * 1024 * 1024),
        cost_estimate=pl.CostEstimate(
            flops=4 * tokens * width * entries,
            bytes_accessed=2 * width * entries + 4 * tokens * width,
            transcendentals=0,
        ),
    )(*grads, *rows_all, *after)


def in_order(first, last, places):
    nx, vb, va, half, cols = first.shape
    block = 2 * half

    def body(places_ref, first_ref, last_ref, out_ref):
        for r in range(nx):
            out_ref[r * block : r * block + half] = first_ref[r, 0, 0]
            out_ref[r * block + half : (r + 1) * block] = last_ref[0, r, 0]

    def first_at(step, at):
        return (0, (step % vb) ^ at[1], (step // vb) ^ at[0], 0, 0)

    def last_at(step, at):
        return ((step % vb) ^ at[1], 0, (step // vb) ^ at[0], 0, 0)

    return pl.pallas_call(
        body,
        grid_spec=pltpu.PrefetchScalarGridSpec(
            num_scalar_prefetch=1,
            grid=(va * vb,),
            in_specs=[
                pl.BlockSpec((nx, 1, 1, half, cols), first_at),
                pl.BlockSpec((1, nx, 1, half, cols), last_at),
            ],
            out_specs=pl.BlockSpec((nx * block, cols), lambda step, at: (0, step)),
        ),
        out_shape=jax.ShapeDtypeStruct((nx * block, va * vb * cols), BF16),
        compiler_params=pltpu.CompilerParams(vmem_limit_bytes=48 * 1024 * 1024),
    )(places, first, last)


def add_after(left, right, after):
    def body(*refs):
        total = refs[0][...].astype(F32) + refs[1][...].astype(F32)
        refs[-1][...] = total.astype(BF16)

    return kernel_call(
        body,
        (1,),
        [whole_block(left.shape)] * 2 + [pl.BlockSpec(memory_space=pl.ANY)] * len(after),
        whole_block(left.shape),
        jax.ShapeDtypeStruct(left.shape, BF16),
        left.size,
        8 * left.size,
    )(left, right, *after)


def held_back(value, after):
    def body(*refs):
        refs[-1][...] = refs[0][...]

    return kernel_call(
        body,
        (1,),
        [whole_block(value.shape)] + [pl.BlockSpec(memory_space=pl.ANY)] * len(after),
        whole_block(value.shape),
        jax.ShapeDtypeStruct(value.shape, value.dtype),
        0,
        2 * value.size * value.dtype.itemsize,
    )(value, *after)


def weight_gradient(normed, proj_grad, weight, after):
    tokens, feat = normed.shape
    cols = proj_grad.shape[1]
    tile = feat // 2 if feat % 256 == 0 and feat // 2 % 128 == 0 else feat

    def body(normed_ref, grad_ref, weight_ref, *rest):
        out_ref, sum_ref = rest[-2:]
        grad = contract_first(normed_ref[...], grad_ref[...])
        out_ref[...] = grad.astype(BF16)
        total = jnp.sum(grad * weight_ref[...].astype(F32), axis=1, keepdims=True)
        sum_ref[...] = jnp.broadcast_to(total, sum_ref.shape)

    out, sums = kernel_call(
        body,
        (feat // tile,),
        [
            pl.BlockSpec((tokens, tile), lambda step: (0, step)),
            whole_block((tokens, cols)),
            pl.BlockSpec((tile, cols), lambda step: (step, 0)),
        ]
        + [pl.BlockSpec(memory_space=pl.ANY)] * len(after),
        [
            pl.BlockSpec((tile, cols), lambda step: (step, 0)),
            pl.BlockSpec((tile, 128), lambda step: (step, 0)),
        ],
        [
            jax.ShapeDtypeStruct((feat, cols), BF16),
            jax.ShapeDtypeStruct((feat, 128), F32),
        ],
        2 * tokens * feat * cols,
        4 * feat * cols + 2 * tokens * (feat + cols),
    )(normed, proj_grad, weight, *after)
    return out, sums[:, 0]


def dot(left, right):
    return jnp.dot(left, right, preferred_element_type=F32)


def cut(array, start, width, axis):
    return lax.dynamic_slice_in_dim(array, start, width, axis)


def local(
    hidden_state,
    embedded_next,
    gain_hidden,
    gain_embed,
    proj_hidden,
    proj_embed,
    final_gain,
    head,
    targets,
    loss_mask,
):
    nc, nv = lax.axis_size("ctx"), lax.axis_size("vocab")
    nx, va = nc // 2, 4
    vb = nv // va
    core = Dim("ctx", nc, 2, 1)
    dim_x = Dim("ctx", nc, nx, 2)
    dim_b = Dim("vocab", nv, vb, 1)
    dim_a = Dim("vocab", nv, va, vb)
    own, slot = lax.axis_index("ctx"), lax.axis_index("vocab")
    x, c, b = own // 2, own % 2, slot % vb

    width = hidden_state.shape[1]
    block = hidden_state.shape[0]
    token_total = targets.shape[0]
    feat, cols = proj_hidden.shape
    half = block // 2
    near = nx * block
    vocab_local = head.shape[0]

    def relative_place(block_index):
        return (c ^ (block_index % 2)) * nx + (x - block_index // 2) % nx

    def block_at(place):
        return ((x - place % nx) % nx) * 2 + (c ^ (place // nx))

    order = jnp.stack([relative_place(jnp.int32(i)) for i in range(nc)])
    to_absolute = (order[:, None] == jnp.arange(nc, dtype=jnp.int32)[None, :])[:, :, None]

    def absolute(value):
        value = value.reshape(value.shape[:-1] + (1, nc, block))
        return jnp.sum(jnp.where(to_absolute, value, 0), axis=-2)

    def relative(value):
        value = jnp.sum(jnp.where(to_absolute, value[..., :, None, :], 0), axis=-3)
        return value.reshape(value.shape[:-2] + (token_total,))

    places = [(rc, rx) for rc in range(2) for rx in range(nx)]

    def send(value, rc, rx):
        pairs = []
        for i in range(nc):
            pairs.append((i, ((i // 2 + rx) % nx) * 2 + ((i % 2) ^ rc)))
        return lax.ppermute(value, "ctx", pairs)

    def scale_of(wide):
        wide = wide.astype(F32)
        return lax.rsqrt(jnp.mean(wide * wide, axis=-1, keepdims=True) + EPSILON)

    def normed_piece(wide, scale, gain, rc, rx):
        start = (((x + rx) % nx) * 2 + (c ^ rc)) * feat
        value = cut(wide, start, feat, 1).astype(F32)
        return (value * scale * cut(gain, start, feat, 0)).astype(BF16)

    hidden_scale, embed_scale = scale_of(hidden_state), scale_of(embedded_next)
    even = b % 2 == 0
    far_h, far_e = {}, {}
    for rx in range(nx):
        for rc in range(2):
            piece_h = normed_piece(hidden_state, hidden_scale, gain_hidden, rc, rx)
            piece_e = normed_piece(embedded_next, embed_scale, gain_embed, rc, rx)
            if rx == 0:
                far_h[rc, 0] = send(piece_h, rc, 0) if rc else piece_h
                far_e[rc, 0] = send(piece_e, rc, 0) if rc else piece_e
                continue
            got = send(jnp.where(even, piece_h, piece_e), rc, rx)
            twin = dim_b.swap(got, 1)
            far_h[rc, rx] = jnp.where(even, got, twin)
            far_e[rc, rx] = jnp.where(even, twin, got)
    blocks_h = [far_h[place] for place in places]
    blocks_e = [far_e[place] for place in places]

    halves_h = [dot(piece, proj_hidden) for piece in blocks_h]
    halves_e = [dot(piece, proj_embed) for piece in blocks_e]
    projected = halves_h[0] + halves_e[0]
    for index, (rc, rx) in enumerate(places[1:], 1):
        term = (halves_h[index] + halves_e[index]).astype(BF16)
        projected = projected + send(term, rc, (nx - rx) % nx).astype(F32)

    piece = (projected * final_gain).astype(BF16)
    squares = jnp.sum(projected * projected, axis=-1)
    squares = lax.all_to_all(
        jnp.broadcast_to(squares, (nc * nv, block)), ("ctx", "vocab"), 0, 0, tiled=True
    )
    squares = jnp.sum(squares.reshape(nc, nv, block), axis=1)
    row_scale = relative(lax.rsqrt(squares / width + EPSILON))
    if cols % 128 == 0:
        far = dim_a.swap(piece, 2)
        near_pair = dim_a.swap(jnp.stack([piece, far]), 1)
        along = jnp.stack([piece, near_pair[0], far, near_pair[1]])
        first, last = along[:, :half], along[:, half:]
        first = jnp.stack([first] + [dim_b.swap(first, r) for r in range(1, vb)])
        last = jnp.stack([last] + [dim_x.turn(last, r) for r in range(1, nx)])
        first = jnp.stack([first] + [dim_x.turn(first, r) for r in range(1, nx)])
        last = jnp.stack([last] + [dim_b.swap(last, r) for r in range(1, vb)])
        rows_near = in_order(first, last, jnp.stack([slot // vb, b]))
        gathered = [rows_near, core.swap(rows_near, 1)]
    else:
        pieces = lax.all_gather(piece, ("ctx", "vocab")).reshape(nc, nv, block, cols)
        lines = [
            lax.dynamic_index_in_dim(pieces, block_at(place), 0, keepdims=False)
            .transpose(1, 0, 2)
            .reshape(block, width)
            for place in range(nc)
        ]
        gathered = [jnp.concatenate(lines[:nx]), jnp.concatenate(lines[nx:])]

    vocab_ids = (own * nv + slot) * vocab_local + lax.iota(jnp.int32, vocab_local)
    target = relative(targets.reshape(nc, block))
    mask_weight = loss_mask.astype(F32).reshape(nc, block)
    mask = relative(mask_weight)
    spans = (slice(0, near), slice(near, token_total))
    logit_halves, target_halves, sums = [], [], []
    for span, rows_half in zip(spans, gathered):
        scale_half = row_scale[span]
        if sums:
            scale_half = held_back(scale_half.reshape(1, near), sums).reshape(near)
        logits = contract_last(rows_half, head) * scale_half[:, None]
        is_target = target[span][:, None] == vocab_ids[None, :]
        power = jnp.exp(logits)
        sums.append(
            jnp.stack(
                [
                    jnp.sum(power, axis=-1),
                    jnp.sum(power * (logits * F32(1.0 / 256.0)), axis=-1),
                    jnp.sum(jnp.where(is_target, logits, F32(0.0)), axis=-1),
                ]
            )
        )
        logit_halves.append(logits)
        target_halves.append(is_target)
    sums = jnp.concatenate(sums, axis=-1)
    exp_total, weighted, target_logit = sum_everywhere(absolute(sums))
    log_total = jnp.log(exp_total)
    mean_loss = jnp.sum(mask_weight * (log_total - target_logit)) / token_total
    scaled_dot = mask * relative(weighted / exp_total * F32(256.0) - target_logit)
    log_rows, weights = relative(log_total)[:, None], (mask * row_scale)[:, None]
    scaled_grads = [
        (
            weights[span] * (jnp.exp(logits - log_rows[span]) - is_target.astype(F32))
        ).astype(BF16)
        for span, logits, is_target in zip(spans, logit_halves, target_halves)
    ]
    coefficient = row_scale * row_scale * scaled_dot / width

    def column_chunk(value, place):
        return jnp.stack([cut(value, (p * vb + place) * cols, cols, 1) for p in range(va)])

    theirs = core.swap(dot(scaled_grads[1], head).astype(BF16), 1)
    mine = lax.optimization_barrier(dot(scaled_grads[0], head).astype(BF16))
    mine = (mine.astype(F32) + theirs.astype(F32)).astype(BF16)
    mine = mine.reshape(nx, block, width)
    first_sends = [mine[r, :half] for r in range(1, nx)]
    last = mine[:, half:].reshape(nx * half, width)
    last_sends = [column_chunk(last, (b + r) % vb) for r in range(1, vb)]
    first_got = [dim_x.turn(value, -r) for r, value in enumerate(first_sends, 1)]
    last = column_chunk(last, b).astype(F32)
    for r, value in enumerate(last_sends, 1):
        last = last + dim_b.turn(value, r).astype(F32)
    grad_head, mark = head_gradient(scaled_grads, gathered, first_sends + last_sends)
    first = add_after(mine[0, :half], first_got[0], [mark])
    for value in first_got[1:]:
        first = (first.astype(F32) + value.astype(F32)).astype(BF16)
    kept = column_chunk(first, b).astype(F32)
    second_sends = [column_chunk(first, (b + r) % vb) for r in range(1, vb)]
    for r, value in enumerate(second_sends, 1):
        kept = kept + dim_b.turn(value, r).astype(F32)
    first = kept.astype(BF16)
    last = last.astype(BF16).reshape(va, nx, half, cols)
    kept = last[:, 0].astype(F32)
    for r in range(1, nx):
        kept = kept + dim_x.turn(last[:, r], -r).astype(F32)
    summed = jnp.concatenate([first, kept.astype(BF16)], axis=1)
    summed = exchange_far(exchange_near(summed, dim_a), dim_a)
    scaled = jnp.concatenate([summed] + [send(summed, rc, rx) for rc, rx in places[1:]])
    scaled = scaled.astype(F32)

    plain = jnp.concatenate([cut(rows_half, slot * cols, cols, 1) for rows_half in gathered])
    plain = plain.astype(F32) / final_gain
    grad_final_gain = jnp.sum(scaled * plain, axis=0)
    proj_grad = (scaled * final_gain - plain * coefficient[:, None]).astype(BF16)

    def final_move(value):
        pairs = []
        ratio = nv // nc
        for i in range(nc):
            for j in range(nv):
                pairs.append((i * nv + j, (j // ratio) * nv + i * ratio + j % ratio))
        return lax.ppermute(value, ("ctx", "vocab"), pairs)

    def products(weight, place):
        picked = jnp.concatenate(
            [
                cut(proj_grad, relative_place((p * vb + place) // 2) * block, block, 0)
                for p in range(va)
            ]
        )
        weight_half = cut(weight, (place % 2) * cols, cols, 0)
        return contract_last(picked, weight_half).reshape(va, block, cols)

    if vb == nv // nc:
        def half_weight(weight, place):
            return cut(weight, place * cols, cols, 0)

        def along_b(weight):
            return [
                dim_b.swap(contract_last(proj_grad, half_weight(weight, b ^ r)).astype(BF16), r)
                for r in range(1, vb)
            ]

        def to_owners(value):
            value = value.reshape(nc, block, cols)
            moved = [
                send(value[index], rc, (nx - rx) % nx)
                for index, (rc, rx) in enumerate(places[1:], 1)
            ]
            return [value[0]] + moved

        def by_holder(pieces):
            at = [(c ^ (i % 2)) * nx + (i // 2 - x) % nx for i in range(nc)]
            stack = jnp.stack(pieces)
            return jnp.stack(
                [lax.dynamic_index_in_dim(stack, at[i], 0, keepdims=False) for i in range(nc)]
            )

        got_h, got_e = along_b(proj_hidden), along_b(proj_embed)
        kept_h = contract_last(proj_grad, half_weight(proj_hidden, b))
        for value in got_h:
            kept_h = kept_h + value.astype(F32)
        kept_h = kept_h.astype(BF16)
        owned_h = to_owners(kept_h)
        pair_h = exchange_near(by_holder(owned_h), dim_a)
        kept_e = contract_last(proj_grad, half_weight(proj_embed, b))
        for value in got_e[1:]:
            kept_e = kept_e + value.astype(F32)
        kept_e = add_after(kept_e, got_e[0], [pair_h[2]])
        owned_e = to_owners(kept_e)
        owned_e[nx] = held_back(owned_e[nx], [pair_h[1]])
        hidden_summed = exchange_far(pair_h, dim_a)
        hidden_back = hidden_summed.astype(F32)
        marks = [kept_h], [pair_h[2]], [owned_e[nx], hidden_summed]
        embed_back = exchange_far(exchange_near(by_holder(owned_e), dim_a), dim_a).astype(F32)
    else:
        got_h, got_e = [
            [dim_b.swap(products(weight, b ^ r).astype(BF16), r) for r in range(1, vb)]
            for weight in (proj_hidden, proj_embed)
        ]
        kept_h, kept_e = products(proj_hidden, b), products(proj_embed, b)
        for value_h, value_e in zip(got_h, got_e):
            kept_h = kept_h + value_h.astype(F32)
            kept_e = kept_e + value_e.astype(F32)
        pair_h = exchange_near(kept_h.astype(BF16), dim_a)
        pair_e = exchange_near(kept_e.astype(BF16), dim_a)
        hidden_back = final_move(exchange_far(pair_h, dim_a)).astype(F32)
        embed_back = final_move(exchange_far(pair_e, dim_a)).astype(F32)
        marks = [proj_grad], [proj_grad], [proj_grad]

    grad_proj_hidden, gain_h = weight_gradient(
        jnp.concatenate(blocks_h), proj_grad, proj_hidden, marks[0]
    )
    grad_proj_embed, gain_e = weight_gradient(
        jnp.concatenate(blocks_e), proj_grad, proj_embed, marks[1]
    )

    wide = lax.optimization_barrier(proj_grad).astype(F32).reshape(nc, block, cols)
    dots = jnp.stack(
        [jnp.sum(wide * jnp.stack(halves), axis=-1) for halves in (halves_h, halves_e)]
    )
    dots = jnp.sum(jnp.where(to_absolute, dots[:, None], 0), axis=2)
    dots = jnp.broadcast_to(dots.transpose(1, 0, 2)[:, None], (nc, nv, 2, block))
    gains = jnp.stack([gain_h, gain_e])
    ratio = nv // nc
    gains = gains.reshape(2, ratio, cols).transpose(1, 0, 2)[None]
    holder = jnp.arange(nc, dtype=jnp.int32)[:, None, None, None] == own
    gains = jnp.where(holder, gains, F32(0.0)).reshape(nv, 2, cols)
    gains = jnp.broadcast_to(gains[None], (nc, nv, 2, cols))
    ends = jnp.concatenate([dots, gains], axis=-1).reshape(nc * nv, 2, block + cols)
    ends = held_back(ends, marks[2])
    ends = jnp.sum(lax.all_to_all(ends, ("ctx", "vocab"), 0, 0, tiled=True), axis=0)

    def finish(kind, source, gain):
        back_all = (hidden_back, embed_back)[kind]
        scale = (hidden_scale, embed_scale)[kind]
        dot_all = ends[kind, :block][:, None]
        source = cut(source, slot * cols, cols, 1).astype(F32)
        gain = cut(gain, slot * cols, cols, 0)
        grad = scale * (back_all * gain) - source * (scale * scale) * (dot_all / width)
        return grad.astype(BF16), ends[kind, block:] / gain

    grad_hidden, grad_gain_hidden = finish(0, hidden_state, gain_hidden)
    grad_embed, grad_gain_embed = finish(1, embedded_next, gain_embed)
    return (
        mean_loss,
        grad_hidden,
        grad_embed,
        grad_gain_hidden,
        grad_gain_embed,
        grad_proj_hidden,
        grad_proj_embed,
        grad_final_gain,
        grad_head,
    )


def solution(mesh):
    in_specs = (
        P("ctx", None),
        P("ctx", None),
        P(),
        P(),
        P("ctx", "vocab"),
        P("ctx", "vocab"),
        P("vocab"),
        P(("ctx", "vocab"), None),
        P(),
        P(),
    )
    out_specs = (
        P(),
        P("ctx", "vocab"),
        P("ctx", "vocab"),
        P("vocab"),
        P("vocab"),
        P("ctx", "vocab"),
        P("ctx", "vocab"),
        P("vocab"),
        P(("ctx", "vocab"), None),
    )
    return jax.shard_map(local, mesh=mesh, in_specs=in_specs, out_specs=out_specs, check_vma=False)
```
